256 devices in a mesh: wide: 32 (over x, z_hi, y), kvh: 8 (over z_lo, core).
Axes of the slice: x: 4, y: 4, z: 8 (z_hi: 2, z_lo: 4; z = z_hi * 4 + z_lo), core: 2. Of those that a mesh axis runs over, the one named last changes fastest.
Arguments:
- prefill_rows: bfloat16 [32768, 5120], P('wide'), may hold values from -6 to 6
- in_gain: float32 [5120], replicated, may hold values from 0.1 to 1.9
- key_weight: bfloat16 [5120, 1024], P(None, 'kvh'), may hold values from -0.078125 to 0.078125
- value_weight: bfloat16 [5120, 1024], P(None, 'kvh'), may hold values from -0.078125 to 0.078125
- key_gain: float32 [128], replicated, may hold values from 0.5 to 8
- query_gain: float32 [128], replicated, may hold values from 0.5 to 8
- block_request: int32 [1024], P('wide'), may hold values from 0 to 15
- block_target: int32 [1024, 1], P('wide'), may hold values from 0 to 31; in each aligned block of 32 rows (0 to 31, 32 to 63, ...) at most 2 rows name the same one
- context_lengths: int32 [16], replicated, may hold values from 1 to 4096, as said below
- kv_cache: bfloat16 [2, 16, 4096, 1024], P(None, None, 'wide', 'kvh'), may hold values from -6 to 6
- decode_queries: bfloat16 [2, 16, 8192], P(None, None, 'kvh')
- decode_partials: float32 [8, 2, 16, 5120], P('kvh'), may hold values from -4 to 4
- decode_residual: float32 [2, 16, 5120], replicated, may hold values from -6 to 6
Outputs:
- attended: bfloat16 [2, 16, 8192], P(None, None, 'kvh')
- new_blocks: bfloat16 [2048, 32, 2, 1024], P('wide', None, None, 'kvh')
- new_tokens: bfloat16 [2, 16, 2, 1024], P(None, None, None, 'kvh')
The draws below stay inside these ranges and needn't reach their ends.
Inputs may be any that keep to these rules, and one draw needn't show every extreme that they name: `block_target`: among the 32 blocks of one group no decode shard is named more than 2 times, a bound that some block reaches. `context_lengths`: some decode row fills all 4096 positions.
All inputs are finite; a program needn't handle non-finite values.
Results may differ from the reference program's by a relative error of at most 0.029.
Values may be sent and summed in bfloat16 or wider, within the bound.
No kernel may reach another device: no remote copies, remote signals or barrier semaphores. Data moves between devices by JAX's collectives and lax.ppermute only.
A program may use at most 64 MiB of HBM per device.

```python
import math
import jax
import jax.numpy as jnp
import numpy as np
from jax import lax

D = 5120
HD = 128
QH = 64
KVH = 8
R = 16
NB = 32
BLK = 32
CAP = 2
TP = 8
CTX = 4096
NALL = 1024
NPRE = 32768
N_WIDE = 32


def norm_gains(key, low, high):
    vectors = jnp.exp(jax.random.uniform(key, (HD,), jnp.float32, math.log(low), math.log(high)))
    return vectors


def draw_key_gain(key, part):
    key = jax.random.fold_in(key, 5)
    return norm_gains(key, 0.5, 3.0)


def draw_query_gain(key, part):
    key = jax.random.fold_in(key, 6)
    return norm_gains(key, 0.5, 3.0)


def draw_decode_queries(key, part):
    key = jax.random.fold_in(key, 7)
    base_key = jax.random.fold_in(key, 0)
    vectors = jax.random.normal(base_key, (2, R, QH, HD), jnp.float32)
    return vectors.reshape(2, R, QH * HD).astype(jnp.bfloat16)


def draw_context_lengths(key, part):
    key = jax.random.fold_in(key, 11)
    length_key, pick_key = jax.random.split(key)
    lengths = jax.random.randint(length_key, (R,), 1, CTX + 1)
    longest = jax.random.randint(pick_key, (), 0, R)
    return jnp.where(jnp.arange(R) == longest, CTX, lengths).astype(jnp.int32)


def touch_ends(drawn, stream_key, smallest, largest):
    spot = [jax.random.randint(jax.random.fold_in(stream_key, axis), (), 0, length) for axis, length in enumerate(drawn.shape)]
    widest = drawn.shape.index(max(drawn.shape))
    beside = spot[:widest] + [(spot[widest] + 1) % drawn.shape[widest]] + spot[widest + 1:]
    return drawn.at[tuple(spot)].set(smallest).at[tuple(beside)].set(largest)


def block_scale(rng, shape, pieces, smallest, largest):
    factor_of, own = 1.0, jax.random.fold_in(rng, 6)
    for position, blocks in pieces:
        draws = jnp.exp(jax.random.uniform(jax.random.fold_in(own, position), (blocks,), jnp.float32, smallest / len(pieces), largest / len(pieces)))
        factor_of = factor_of * jnp.repeat(draws, shape[position] // blocks).reshape([-1 if axis == position else 1 for axis in range(len(shape))])
    return factor_of


def shared_out(rng, own, number, rows, amount, top, most, slope):
    order = jax.random.permutation(rng, amount)
    heavy_load, common = shares(amount, rows * top, most, slope, True), shares(amount, rows * top, most, slope, False)
    places = jnp.arange(amount)

    def named(sizes, turn):
        used = int((sizes > 0).sum())
        fixed = max(1, used // 4)
        passed = fixed + (places - fixed + turn * (used - fixed)) % max(1, amount - fixed)
        return jnp.zeros((amount,), jnp.int32).at[order[jnp.where(places < fixed, places, passed)]].set(jnp.asarray(sizes, jnp.int32))

    sizes = jnp.where(number % 4 == 0, named(heavy_load, number // 4), named(common, number - number // 4 - 1))
    mixed = jax.random.permutation(jax.random.fold_in(own, 3), amount)
    giver, receiver = mixed[0:amount // 2 * 2:2], mixed[1:amount // 2 * 2:2]
    margin = jnp.minimum(sizes[giver] - 1, most - sizes[receiver]) // 2
    margin = jnp.where((giver == order[0]) | (receiver == order[0]) | (sizes[receiver] == 0), 0, jnp.maximum(margin, 0))
    passed = jax.random.randint(jax.random.fold_in(own, 4), (amount // 2,), 0, 1 << 20) % (margin + 1)
    sizes = sizes.at[giver].add(-passed).at[receiver].add(passed)
    members = jnp.searchsorted(jnp.cumsum(sizes), jnp.arange(rows * top), side="right").astype(jnp.int32)
    listing = members.reshape(top, rows).T
    listing = listing[jax.random.permutation(jax.random.fold_in(own, 1), rows)]
    turn = jax.random.randint(jax.random.fold_in(own, 2), (rows, 1), 0, top)
    return jnp.take_along_axis(listing, (jnp.arange(top)[None, :] + turn) % top, axis=1)


def shares(amount, total, limit, skew, full):
    weights = [(1 << 20) // math.isqrt(standing ** skew) + 1 for standing in range(1, amount + 1)]
    largest = limit if full else min(limit, max(-(-total // amount), total * weights[0] // sum(weights)))
    least = 1 if total - largest >= amount - 1 else 0
    given, spare = [largest] + [least] * (amount - 1), total - largest - least * (amount - 1)
    while spare > 0:
        candidates = [i for i in range(1, amount) if given[i] < largest] or [i for i in range(1, amount) if given[i] < limit]
        whole, left = sum([weights[i] for i in candidates]), spare
        for i in candidates:
            addition = min(limit - given[i], max(1, left * weights[i] // whole), spare)
            given[i] = given[i] + addition
            spare = spare - addition
    return np.array(given)


def gaussian(stream_key, dims, width, reach, cuts=(), kind=jnp.bfloat16):
    result = jax.random.normal(stream_key, dims, jnp.float32) * width
    if len(cuts) > 0:
        result = block_scale(stream_key, dims, cuts, -0.22, 0.18) * result
    return jnp.clip(result, min=-reach, max=reach).astype(kind)


def setup_inputs(seed: int = 0) -> dict:
    key_list = jax.random.split(jax.random.key(seed), 14)
    prefill_rows = gaussian(key_list[0], (NPRE, D), 1.0, 6.0, ((0, 32),))
    in_gain = jnp.clip(1.0 + 0.18 * jax.random.normal(key_list[1], (D,), jnp.float32), 0.1, 1.9)
    key_weight = gaussian(key_list[2], (D, KVH * HD), D ** -0.5, 0.078125, ((1, 8),))
    value_weight = gaussian(key_list[3], (D, KVH * HD), D ** -0.5, 0.078125, ((1, 8),))
    key_gain = draw_key_gain(jax.random.fold_in(key_list[13], 71), 0)
    query_gain = draw_query_gain(jax.random.fold_in(key_list[13], 71), 0)
    block_request = touch_ends(jax.random.randint(key_list[6], (NALL,), 0, R), jax.random.fold_in(key_list[6], 1), 0, R - 1).astype(jnp.int32)
    block_target_keys = jax.random.split(jax.random.fold_in(key_list[7], 1), NALL // NB)
    block_target_turns = jax.random.permutation(jax.random.fold_in(key_list[7], 3), NALL // NB)
    block_target = jax.vmap(lambda own, number: shared_out(jax.random.fold_in(key_list[7], 2), own, number, NB, N_WIDE, 1, CAP, 2))(block_target_keys, block_target_turns).reshape((NALL, 1))
    context_lengths = draw_context_lengths(jax.random.fold_in(key_list[13], 71), 0)
    kv_cache = gaussian(key_list[9], (2, R, CTX, KVH * HD), 1.0, 6.0, ((2, 32), (3, 8)))
    decode_queries = draw_decode_queries(jax.random.fold_in(key_list[13], 71), 0)
    decode_partials = gaussian(key_list[11], (TP, 2, R, D), 0.5, 4.0, ((0, 8),), jnp.float32)
    decode_residual = gaussian(key_list[12], (2, R, D), 1.0, 6.0, (), jnp.float32)
    return {"prefill_rows": prefill_rows, "in_gain": in_gain, "key_weight": key_weight, "value_weight": value_weight, "key_gain": key_gain, "query_gain": query_gain, "block_request": block_request, "block_target": block_target, "context_lengths": context_lengths, "kv_cache": kv_cache, "decode_queries": decode_queries, "decode_partials": decode_partials, "decode_residual": decode_residual}


EPS = 1e-06
THETA = 1000000.0

def head_norm(vectors, gain_vec):
    mean_square = lax.optimization_barrier(jnp.mean(vectors * vectors, axis=-1, keepdims=True))
    return vectors * lax.rsqrt(mean_square + EPS) * gain_vec

def rotate(vectors, positions):
    half_dim = vectors.shape[-1] // 2
    exponent = jnp.arange(half_dim, dtype=jnp.float32) * (2.0 / vectors.shape[-1])
    frequency = jnp.power(jnp.float32(THETA), -exponent)
    angles = positions.astype(jnp.float32)[..., None] * frequency
    cosine = jnp.cos(angles)
    sine_part = jnp.sin(angles)
    front = vectors[..., :half_dim]
    back = vectors[..., half_dim:]
    return jnp.concatenate([front * cosine - back * sine_part, back * cosine + front * sine_part], axis=-1)

def row_norm(hidden, gain_vec):
    mean_square = lax.optimization_barrier(jnp.mean(hidden * hidden, axis=-1, keepdims=True))
    return (hidden * lax.rsqrt(mean_square + EPS) * gain_vec).astype(jnp.bfloat16)

def reference(prefill_rows, in_gain, key_weight, value_weight, key_gain, query_gain, block_request, block_target, context_lengths, kv_cache, decode_queries, decode_partials, decode_residual):
    all_blocks = N_WIDE * NB
    lane_width = KVH * HD
    per_group = QH // KVH
    requests = jnp.arange(R, dtype=jnp.int32)
    owner_table = (block_request[:, None] == requests[None, :]).astype(jnp.int32)
    block_rank = lax.optimization_barrier(jnp.sum((jnp.cumsum(owner_table, axis=0) - owner_table) * owner_table, axis=1))
    counts = lax.optimization_barrier(jnp.sum(owner_table, axis=0))
    block_start = lax.optimization_barrier(jnp.sum(owner_table * context_lengths[None, :], axis=1)) + BLK * block_rank
    token_pos = (block_start[:, None] + jnp.arange(BLK, dtype=jnp.int32)[None, :]).reshape(all_blocks * BLK)
    normed = row_norm(prefill_rows.astype(jnp.float32), in_gain)
    projected = jnp.dot(normed, key_weight, preferred_element_type=jnp.float32).reshape(all_blocks * BLK, KVH, HD)
    prefill_keys = rotate(head_norm(projected, key_gain), token_pos[:, None]).astype(jnp.bfloat16)
    prefill_values = jnp.dot(normed, value_weight, preferred_element_type=jnp.float32).astype(jnp.bfloat16)
    target = block_target[:, 0]
    shards = jnp.arange(N_WIDE, dtype=jnp.int32)
    sent_table = (target[:, None] == shards[None, :]).astype(jnp.int32).reshape(N_WIDE, NB, N_WIDE)
    target_rank = lax.optimization_barrier(jnp.sum((jnp.cumsum(sent_table, axis=1) - sent_table) * sent_table, axis=2)).reshape(all_blocks)
    source = jnp.arange(all_blocks, dtype=jnp.int32) // NB
    slot_index = target * (N_WIDE * CAP) + source * CAP + target_rank
    blocks = jnp.stack([prefill_keys.reshape(all_blocks, BLK, lane_width), prefill_values.reshape(all_blocks, BLK, lane_width)], axis=2)
    new_blocks = jnp.zeros((N_WIDE * N_WIDE * CAP, BLK, 2, lane_width), jnp.bfloat16).at[slot_index].set(blocks)
    hidden = decode_residual + lax.optimization_barrier(jnp.sum(decode_partials, axis=0))
    decode_normed = row_norm(hidden, in_gain)
    decode_pos = (context_lengths + BLK * counts)[None, :] + jnp.arange(2, dtype=jnp.int32)[:, None]
    flat_rows = decode_normed.reshape(2 * R, D)
    new_proj = jnp.dot(flat_rows, key_weight, preferred_element_type=jnp.float32).reshape(2, R, KVH, HD)
    new_keys = rotate(head_norm(new_proj, key_gain), decode_pos[:, :, None]).astype(jnp.bfloat16)
    new_values = jnp.dot(flat_rows, value_weight, preferred_element_type=jnp.float32).astype(jnp.bfloat16).reshape(2, R, lane_width)
    new_tokens = jnp.stack([new_keys.reshape(2, R, lane_width), new_values], axis=2)
    query_heads = decode_queries.astype(jnp.float32).reshape(2, R, QH, HD)
    queries = rotate(head_norm(query_heads, query_gain), decode_pos[:, :, None]).astype(jnp.bfloat16)
    score_scale = HD ** (-0.5)
    live_cache = jnp.arange(CTX, dtype=jnp.int32)[None, :] < context_lengths[:, None]
    live_block = jnp.repeat(block_request, BLK)[None, :] == requests[:, None]
    causal = jnp.arange(2)[:, None] >= jnp.arange(2)[None, :]
    outputs = []
    for kv_head in range(KVH):
        low = kv_head * HD
        query_part = queries[:, :, kv_head * per_group:(kv_head + 1) * per_group].astype(jnp.float32)
        cache_keys = kv_cache[0, :, :, low:low + HD].astype(jnp.float32)
        cache_values = kv_cache[1, :, :, low:low + HD].astype(jnp.float32)
        block_keys = prefill_keys[:, kv_head].astype(jnp.float32)
        block_values = prefill_values[:, low:low + HD].astype(jnp.float32)
        own_keys = new_keys[:, :, kv_head].astype(jnp.float32)
        own_values = new_values[:, :, low:low + HD].astype(jnp.float32)
        cache_scores = jnp.einsum('srgd,rcd->srgc', query_part, cache_keys) * score_scale
        block_scores = jnp.einsum('srgd,nd->srgn', query_part, block_keys) * score_scale
        own_scores = jnp.einsum('srgd,trd->srgt', query_part, own_keys) * score_scale
        cache_mask = live_cache[None, :, None, :]
        block_mask = live_block[None, :, None, :]
        own_mask = causal[:, None, None, :]
        row_top = jnp.maximum(jnp.maximum(lax.optimization_barrier(jnp.max(jnp.where(cache_mask, cache_scores, -jnp.inf), axis=-1)), lax.optimization_barrier(jnp.max(jnp.where(block_mask, block_scores, -jnp.inf), axis=-1))), lax.optimization_barrier(jnp.max(jnp.where(own_mask, own_scores, -jnp.inf), axis=-1)))
        cache_weights = jnp.where(cache_mask, jnp.exp(cache_scores - row_top[..., None]), 0.0)
        block_weights = jnp.where(block_mask, jnp.exp(block_scores - row_top[..., None]), 0.0)
        own_weights = jnp.where(own_mask, jnp.exp(own_scores - row_top[..., None]), 0.0)
        row_total = lax.optimization_barrier(jnp.sum(cache_weights, axis=-1)) + lax.optimization_barrier(jnp.sum(block_weights, axis=-1)) + lax.optimization_barrier(jnp.sum(own_weights, axis=-1))
        weighted = jnp.einsum('srgc,rcd->srgd', cache_weights.astype(jnp.bfloat16).astype(jnp.float32), cache_values)
        weighted = weighted + jnp.einsum('srgn,nd->srgd', block_weights.astype(jnp.bfloat16).astype(jnp.float32), block_values)
        weighted = weighted + jnp.einsum('srgt,trd->srgd', own_weights.astype(jnp.bfloat16).astype(jnp.float32), own_values)
        outputs.append(weighted / row_total[..., None])
    attended = jnp.concatenate(outputs, axis=2).reshape(2, R, QH * HD).astype(jnp.bfloat16)
    return (attended, new_blocks, new_tokens)
```

```python
import functools

import jax
import jax.numpy as jnp
import numpy as np
from jax import lax
from jax.experimental import pallas as pl
from jax.experimental.pallas import tpu as pltpu
from jax.sharding import PartitionSpec as P

CAP = 2
EPS = 1e-06
THETA = 1000000.0
MASKED = -3e38
FLOOR = -1e30
F32 = jnp.float32
BF16 = jnp.bfloat16
VMEM_LIMIT = 48 * 1024 * 1024

HD = 128
BLK = 32
STAT = 256
TOK = 272
ROWS = 336


def params(**kw):
    return pltpu.CompilerParams(vmem_limit_bytes=VMEM_LIMIT, **kw)


def dot(a, b):
    return jnp.dot(a, b, preferred_element_type=F32)


def dot_nt(a, b):
    return lax.dot_general(a, b, (((1,), (1,)), ((), ())), preferred_element_type=F32)


def rope_sign():
    lane = lax.broadcasted_iota(jnp.int32, (1, HD), 1)
    return jnp.where(lane < HD // 2, -1.0, 1.0).astype(F32)


def head_norm(x, gain):
    return x * lax.rsqrt(jnp.mean(x * x, axis=-1, keepdims=True) + EPS) * gain


def project_kernel(x_ref, gain_ref, wk_ref, wv_ref, kgain_ref, k_ref, v_ref, w_ref):
    depth = x_ref.shape[1]
    chunk = 512

    @pl.when(pl.program_id(0) == 0)
    def _():
        w_ref[:, :HD] = wk_ref[...]
        w_ref[:, HD:] = wv_ref[...]

    rows = x_ref.shape[0]
    acc = jnp.zeros((rows, 2 * HD), F32)
    squares = jnp.zeros((rows, HD), F32)
    for start in range(0, depth, chunk):
        x = x_ref[:, start : start + chunk].astype(F32)
        sq = x * x
        for part in range(0, chunk, HD):
            squares = squares + sq[:, part : part + HD]
        y = (x * gain_ref[:, start : start + chunk]).astype(BF16)
        acc = acc + dot(y, w_ref[start : start + chunk, :])
    scale = lax.rsqrt(jnp.sum(squares, axis=1, keepdims=True) * (1.0 / depth) + EPS)
    acc = acc * scale
    k_ref[...] = head_norm(acc[:, :HD], kgain_ref[...])
    v_ref[...] = acc[:, HD:].astype(BF16)


def project(rows, gain, wk, wv, kgain):
    count, depth = rows.shape
    tile = 256
    return pl.pallas_call(
        project_kernel,
        grid=(count // tile,),
        in_specs=[
            pl.BlockSpec((tile, depth), lambda i: (i, 0)),
            pl.BlockSpec((1, depth), lambda i: (0, 0)),
            pl.BlockSpec((depth, HD), lambda i: (0, 0)),
            pl.BlockSpec((depth, HD), lambda i: (0, 0)),
            pl.BlockSpec((1, HD), lambda i: (0, 0)),
        ],
        out_specs=[
            pl.BlockSpec((tile, HD), lambda i: (i, 0)),
            pl.BlockSpec((tile, HD), lambda i: (i, 0)),
        ],
        out_shape=[
            jax.ShapeDtypeStruct((count, HD), F32),
            jax.ShapeDtypeStruct((count, HD), BF16),
        ],
        scratch_shapes=[pltpu.VMEM((depth, 2 * HD), BF16)],
        compiler_params=params(),
        cost_estimate=pl.CostEstimate(
            flops=4 * count * depth * HD, bytes_accessed=2 * count * depth, transcendentals=0
        ),
        name="project",
    )(rows, gain, wk, wv, kgain)


def pack_kernel(slot_ref, k_ref, v_ref, ang_ref, ct_ref, st_ref, perm_ref, kr_ref, out_ref):
    sign = rope_sign()
    ang = ang_ref[...]
    cb, sb = jnp.cos(ang), jnp.sin(ang)
    ct, st = ct_ref[...], st_ref[...]
    perm = perm_ref[...]
    out_ref[...] = jnp.zeros(out_ref.shape, BF16)
    for b in range(slot_ref.shape[0]):
        rows = slice(b * BLK, (b + 1) * BLK)
        c1, s1 = cb[b : b + 1], sb[b : b + 1]
        c = c1 * ct - s1 * st
        s = (s1 * ct + c1 * st) * sign
        k = k_ref[rows, :]
        kr = (k * c + pltpu.roll(k, HD // 2, 1) * s).astype(BF16)
        kr_ref[rows, :] = kr
        both = jnp.concatenate([kr, v_ref[rows, :]], axis=0)
        place = pl.multiple_of(slot_ref[b] * (2 * BLK), 2 * BLK)
        out_ref[pl.ds(place, 2 * BLK), :] = dot(perm, both).astype(BF16)


def pack(slots, keys, values, angles, ct, st, perm, slot_count):
    vmem = pl.BlockSpec(memory_space=pltpu.VMEM)
    return pl.pallas_call(
        pack_kernel,
        in_specs=[pl.BlockSpec(memory_space=pltpu.SMEM)] + [vmem] * 6,
        out_specs=[vmem, vmem],
        out_shape=[
            jax.ShapeDtypeStruct(keys.shape, BF16),
            jax.ShapeDtypeStruct((slot_count * 2 * BLK, HD), BF16),
        ],
        compiler_params=params(),
        cost_estimate=pl.CostEstimate(
            flops=40_000_000, bytes_accessed=2_500_000, transcendentals=0
        ),
        name="pack",
    )(slots, keys, values, angles, ct, st, perm)


def token_kernel(row_ref, a_ref, b_ref, res_ref, gain_ref, wk_ref, wv_ref, kgain_ref, ang_ref, out_ref):
    hidden = res_ref[...] + (a_ref[...].astype(F32) + b_ref[...].astype(F32))
    scale = lax.rsqrt(jnp.mean(hidden * hidden, axis=-1, keepdims=True) + EPS)
    normed = hidden * scale * gain_ref[...]
    wide = jnp.broadcast_to(normed, (16, normed.shape[1])).astype(BF16)
    k = head_norm(dot(wide, wk_ref[...]), kgain_ref[...])
    ang = ang_ref[...]
    k = k * jnp.cos(ang) + pltpu.roll(k, HD // 2, 1) * (jnp.sin(ang) * rope_sign())
    v = dot(wide, wv_ref[...])
    both = jnp.concatenate([k, k, v, v], axis=0)
    row = lax.broadcasted_iota(jnp.int32, both.shape, 0) % 32
    out_ref[...] = jnp.where(row == row_ref[0], both, 0.0).astype(BF16)


def token(row, a, b, res, gain, wk, wv, kgain, ang):
    vmem = pl.BlockSpec(memory_space=pltpu.VMEM)
    return pl.pallas_call(
        token_kernel,
        in_specs=[pl.BlockSpec(memory_space=pltpu.SMEM)] + [vmem] * 8,
        out_specs=vmem,
        out_shape=jax.ShapeDtypeStruct((64, HD), BF16),
        compiler_params=params(),
        cost_estimate=pl.CostEstimate(
            flops=50_000_000, bytes_accessed=3_000_000, transcendentals=0
        ),
        name="token",
    )(row, a, b, res, gain, wk, wv, kgain, ang)


def put_stats(ref, c, total):
    hi = total.astype(BF16).astype(F32)
    stats = jnp.concatenate([c, hi, total - hi, jnp.zeros((10, HD), F32)], axis=0)
    ref[STAT:TOK, :] = stats.astype(BF16)


def attend_kernel(
    limit_ref, q_ref, qgain_ref, ang_ref, kr_ref, v_ref, cache_ref, owner_ref, tok_ref,
    out_ref, qr_ref, q_scr, s_scr, o_scr,
):
    heads = q_ref.shape[1] // HD
    rows = cache_ref.shape[1]
    pairs = q_ref.shape[0]
    queries = heads * pairs
    per_row = queries // rows
    score_scale = HD ** (-0.5)
    ang = ang_ref[...]
    cd, sd = jnp.cos(ang), jnp.sin(ang) * rope_sign()
    for h in range(heads):
        x = head_norm(q_ref[:, h * HD : (h + 1) * HD].astype(F32), qgain_ref[...])
        qr = (x * cd + pltpu.roll(x, HD // 2, 1) * sd).astype(BF16)
        qr_ref[h * pairs : (h + 1) * pairs, :] = qr
        q_scr[h * pairs : (h + 1) * pairs, :] = qr.astype(F32)
    lane = lax.broadcasted_iota(jnp.int32, (per_row, HD), 1)
    for r in range(rows):
        mine = pl.ds(r, per_row, stride=rows)
        s = dot_nt(q_scr[mine, :].astype(BF16), cache_ref[0, r]) * score_scale
        s_scr[mine, :] = jnp.where(lane < limit_ref[r], s, MASKED)
    block = dot_nt(qr_ref[...], kr_ref[...]) * score_scale
    row = lax.broadcasted_iota(jnp.int32, (queries, 1), 0) % rows
    block = jnp.where(row == owner_ref[...], block, MASKED)
    cache = s_scr[...]
    top = jnp.maximum(
        jnp.max(cache, axis=1, keepdims=True), jnp.max(block, axis=1, keepdims=True)
    )
    c = jnp.maximum(top, FLOOR).astype(BF16).astype(F32)
    cache = jnp.exp(cache - c)
    block = jnp.exp(block - c)
    total = jnp.sum(cache, axis=1, keepdims=True) + jnp.sum(block, axis=1, keepdims=True)
    s_scr[...] = cache
    for r in range(rows):
        mine = pl.ds(r, per_row, stride=rows)
        o_scr[mine, :] = dot(s_scr[mine, :].astype(BF16), cache_ref[1, r])
    out_ref[:STAT, :] = (dot(block.astype(BF16), v_ref[...]) + o_scr[...]).astype(BF16)
    lane = lax.broadcasted_iota(jnp.int32, (queries, HD), 1)
    both = jnp.where(lane == 0, c, jnp.where(lane == 1, total, 0.0))
    t0, t1 = both[:HD].T, both[HD:].T
    put_stats(
        out_ref,
        jnp.concatenate([t0[0:1], t1[0:1]], axis=0),
        jnp.concatenate([t0[1:2], t1[1:2]], axis=0),
    )
    out_ref[TOK:, :] = tok_ref[...]


def attend(limit, q, qgain, ang, kr, v, cache, owner, tok):
    vmem = pl.BlockSpec(memory_space=pltpu.VMEM)
    return pl.pallas_call(
        attend_kernel,
        in_specs=[pl.BlockSpec(memory_space=pltpu.SMEM)] + [vmem] * 8,
        out_specs=[vmem, vmem],
        out_shape=[
            jax.ShapeDtypeStruct((ROWS, HD), BF16),
            jax.ShapeDtypeStruct((STAT, HD), BF16),
        ],
        scratch_shapes=[pltpu.VMEM((STAT, HD), F32)] * 3,
        compiler_params=params(),
        cost_estimate=pl.CostEstimate(
            flops=400_000_000, bytes_accessed=3_000_000, transcendentals=300_000
        ),
        name="attend",
    )(limit, q, qgain, ang, kr, v, cache, owner, tok)


def merged(refs):
    cs = [ref[STAT : STAT + 2, :].astype(F32) for ref in refs]
    top = functools.reduce(jnp.maximum, cs)
    factors = [jnp.exp(c - top) for c in cs]
    total = jnp.zeros_like(top)
    for ref, f in zip(refs, factors):
        stats = ref[STAT:TOK, :].astype(F32)
        total = total + f * (stats[2:4] + stats[4:6])
    pad = jnp.zeros((HD - 2 * len(refs), HD), F32)
    cols = jnp.concatenate(factors + [pad], axis=0).T
    halves = []
    for g in range(2):
        acc = None
        for i, ref in enumerate(refs):
            term = ref[g * HD : (g + 1) * HD, :].astype(F32) * cols[:, 2 * i + g : 2 * i + g + 1]
            acc = term if acc is None else acc + term
        halves.append(acc)
    tok = functools.reduce(lambda a, b: a + b, [ref[TOK:, :].astype(F32) for ref in refs])
    return halves, top, total, tok


def merge_kernel(*refs):
    out_ref = refs[-1]
    halves, top, total, tok = merged(refs[:-1])
    for g in range(2):
        out_ref[g * HD : (g + 1) * HD, :] = halves[g].astype(BF16)
    put_stats(out_ref, top, total)
    out_ref[TOK:, :] = tok.astype(BF16)


def merge(parts):
    vmem = pl.BlockSpec(memory_space=pltpu.VMEM)
    return pl.pallas_call(
        merge_kernel,
        in_specs=[vmem] * len(parts),
        out_specs=vmem,
        out_shape=jax.ShapeDtypeStruct((ROWS, HD), BF16),
        compiler_params=params(),
        name="merge",
    )(*parts)


def final_kernel(qr_ref, perm_ref, *refs):
    out_ref, tok_out_ref = refs[-2:]
    halves, top, total, tok = merged(refs[:-2])
    tok = tok.astype(BF16)
    tok_out_ref[...] = dot(perm_ref[...], tok).astype(BF16)
    new_k, new_v = tok[:32], tok[32:]
    pad = jnp.zeros((HD - 4, HD), F32)
    cols = jnp.concatenate([top, total, pad], axis=0).T
    col = lax.broadcasted_iota(jnp.int32, (HD, 32), 1)
    row = lax.broadcasted_iota(jnp.int32, (HD, 32), 0)
    same = (col % 16 == row % 16) & (col // 16 <= (row // 16) % 2)
    for g in range(2):
        s = dot_nt(qr_ref[g * HD : (g + 1) * HD, :], new_k) * (HD ** (-0.5))
        s = jnp.where(same, s, MASKED)
        c, old = cols[:, g : g + 1], cols[:, 2 + g : 3 + g]
        m = jnp.maximum(c, jnp.max(s, axis=1, keepdims=True))
        f = jnp.exp(c - m)
        p = jnp.exp(s - m)
        whole = old * f + jnp.sum(p, axis=1, keepdims=True)
        o = ((halves[g] * f + dot(p.astype(BF16), new_v)) / whole).astype(BF16)
        for h in range(4):
            head = g * 4 + h
            out_ref[:, head * HD : (head + 1) * HD] = o[h * 32 : (h + 1) * 32]


def final(qr, perm, parts):
    vmem = pl.BlockSpec(memory_space=pltpu.VMEM)
    return pl.pallas_call(
        final_kernel,
        in_specs=[vmem] * (2 + len(parts)),
        out_specs=[vmem, vmem],
        out_shape=[
            jax.ShapeDtypeStruct((32, 8 * HD), BF16),
            jax.ShapeDtypeStruct((64, HD), BF16),
        ],
        compiler_params=params(),
        name="final",
    )(qr, perm, *parts)


Y_STEPS, Z_STEPS, X_STEPS = (1, 2, 3), (4,), (8, 16, 24)


def exchange(value, axis, steps):
    size = lax.axis_size(axis)
    return [lax.ppermute(value, axis, [(i, i ^ m) for i in range(size)]) for m in steps]


def local(
    prefill_rows,
    in_gain,
    key_weight,
    value_weight,
    key_gain,
    query_gain,
    block_request,
    block_target,
    context_lengths,
    kv_cache,
    decode_queries,
    decode_partials,
    decode_residual,
):
    me = lax.axis_index("wide")
    wide_count = lax.axis_size("wide")
    depth = prefill_rows.shape[1]
    row_count = context_lengths.shape[0]
    slot_count = kv_cache.shape[2]

    frequency = np.tile(THETA ** (-np.arange(HD // 2) / (HD // 2)), 2)
    offsets = np.arange(BLK)[:, None] * frequency[None, :]
    ct = jnp.asarray(np.cos(offsets), F32)
    st = jnp.asarray(np.sin(offsets), F32)
    freq = jnp.asarray(frequency, F32)
    perm_np = np.zeros((2 * BLK, 2 * BLK), np.float32)
    for i in range(BLK):
        perm_np[2 * i, i] = 1
        perm_np[2 * i + 1, BLK + i] = 1
    perm = jnp.asarray(perm_np, BF16)

    requests = jnp.arange(row_count, dtype=jnp.int32)
    owned = (block_request[:, None] == requests[None, :]).astype(jnp.int32)
    total = jnp.sum(owned, axis=0)
    ahead = jnp.zeros_like(total)
    for steps in (Y_STEPS, Z_STEPS, X_STEPS):
        others = exchange(total, "wide", steps)
        for m, other in zip(steps, others):
            ahead = ahead + jnp.where((me ^ m) < me, other, 0)
            total = total + other

    token_index, request_index = me // row_count, me % row_count
    part = lax.dynamic_slice(
        decode_partials, (0, token_index, request_index, 0), (1, 1, 1, depth)
    ).reshape(1, depth)
    part = part.astype(BF16)
    for m in (1, 2):
        (other,) = exchange(part, "kvh", (m,))
        part = (part.astype(F32) + other.astype(F32)).astype(BF16)
    (other,) = exchange(part, "kvh", (4,))
    residual = lax.dynamic_slice(
        decode_residual, (token_index, request_index, 0), (1, 1, depth)
    ).reshape(1, depth)

    keys, values = project(
        prefill_rows, in_gain.reshape(1, depth), key_weight, value_weight, key_gain.reshape(1, HD)
    )

    earlier = jnp.arange(BLK)[None, :] < jnp.arange(BLK)[:, None]
    rank = jnp.sum((block_request[:, None] == block_request[None, :]) & earlier, axis=1)
    start = jnp.sum(owned * (context_lengths + BLK * ahead)[None, :], axis=1) + BLK * rank
    angles = start.astype(F32)[:, None] * freq[None, :]
    target = block_target[:, 0]
    target_rank = jnp.sum((target[:, None] == target[None, :]) & earlier, axis=1)
    slots = (target * CAP + target_rank).astype(jnp.int32)
    decode_pos = (context_lengths + BLK * total)[None, :] + jnp.arange(2, dtype=jnp.int32)[:, None]
    decode_angles = decode_pos.reshape(-1).astype(F32)[:, None] * freq[None, :]
    my_angle = (
        jnp.sum(jnp.where(requests == request_index, context_lengths + BLK * total, 0))
        + token_index
    ).astype(F32) * freq[None, :]

    rotated, outgoing = pack(slots, keys, values, angles, ct, st, perm, wide_count * CAP)
    received = lax.all_to_all(
        outgoing.reshape(wide_count, CAP * 2 * BLK, HD),
        "wide",
        split_axis=0,
        concat_axis=0,
        tiled=True,
    )
    new_blocks = received.reshape(wide_count * CAP, BLK, 2, HD)

    tok = token(
        me.astype(jnp.int32).reshape(1), part, other, residual, in_gain.reshape(1, depth),
        key_weight, value_weight, key_gain.reshape(1, HD), my_angle,
    )
    limit = context_lengths - me * slot_count
    owner = jnp.repeat(block_request, BLK).reshape(1, -1)
    payload, queries = attend(
        limit, decode_queries.reshape(2 * row_count, -1), query_gain.reshape(1, HD), decode_angles,
        rotated, values, kv_cache, owner, tok,
    )
    payload = merge([payload] + exchange(payload, "wide", Y_STEPS))
    payload = merge([payload] + exchange(payload, "wide", Z_STEPS))
    attended, tokens = final(queries, perm, [payload] + exchange(payload, "wide", X_STEPS))
    return (
        attended.reshape(2, row_count, -1),
        new_blocks,
        tokens.reshape(2, row_count, 2, HD),
    )


def solution(mesh):
    placed = (
        P("wide", None),
        P(),
        P(None, "kvh"),
        P(None, "kvh"),
        P(),
        P(),
        P("wide"),
        P("wide", None),
        P(),
        P(None, None, "wide", "kvh"),
        P(None, None, "kvh"),
        P("kvh", None, None, None),
        P(),
    )
    return jax.shard_map(
        local,
        mesh=mesh,
        in_specs=placed,
        out_specs=(P(None, None, "kvh"), P("wide", None, None, "kvh"), P(None, None, None, "kvh")),
        check_vma=False,
    )
```

```python
import functools

import jax
import jax.numpy as jnp
import numpy as np
from jax import lax
from jax.experimental import pallas as pl
from jax.experimental.pallas import tpu as pltpu
from jax.sharding import PartitionSpec as P

CAP = 2
EPS = 1e-06
THETA = 1000000.0
MASKED = -3e38
FLOOR = -1e30
F32 = jnp.float32
BF16 = jnp.bfloat16

HD = 128
BLK = 32
STAT = 256
STAGES = ((1, 2, 3), (8, 16, 24), (4,))


def params(limit=16):
    return pltpu.CompilerParams(vmem_limit_bytes=limit * 1024 * 1024)


VMEM = pl.BlockSpec(memory_space=pltpu.VMEM)
SMEM = pl.BlockSpec(memory_space=pltpu.SMEM)
HBM = pl.BlockSpec(memory_space=pltpu.HBM)


def dot(a, b):
    return jnp.dot(a, b, preferred_element_type=F32)


def dot_nt(a, b):
    return lax.dot_general(a, b, (((1,), (1,)), ((), ())), preferred_element_type=F32)


def iota(shape, axis):
    return lax.broadcasted_iota(jnp.int32, shape, axis)


def rope_sign():
    return jnp.where(iota((1, HD), 1) < HD // 2, -1.0, 1.0).astype(F32)


def head_norm(x, gain):
    return x * lax.rsqrt(jnp.mean(x * x, axis=-1, keepdims=True) + EPS) * gain


def one_hot_rows(req_ref, scr):
    lane = iota((1, HD), 1)
    for b in range(BLK):
        scr[b : b + 1, :] = jnp.where(lane == req_ref[b], 1.0, 0.0)
    return scr[...]


def stay(*arrays):
    return [pltpu.with_memory_space_constraint(x, pltpu.HBM) for x in arrays]


def start_all(pairs, sems):
    copies = [pltpu.make_async_copy(src, dst, sems.at[i]) for i, (src, dst) in enumerate(pairs)]
    for copy in copies:
        copy.start()
    return copies


def wait_all(copies):
    for copy in copies:
        copy.wait()


def tile_of_rows(ref, me, rows):
    return ref.at[me // rows, pl.ds(pl.multiple_of(me % rows // 8 * 8, 8), 8), :]


def meta_kernel(req_hbm, target_hbm, out_ref, place_ref, req_ref, target_ref, hot_ref, used_ref, seen_ref, sems):
    copies = start_all([(req_hbm, req_ref), (target_hbm, target_ref)], sems)
    wide_count = out_ref.shape[0]
    for d in range(wide_count):
        used_ref[d] = 0
        seen_ref[d] = 0
    out_ref[...] = jnp.zeros(out_ref.shape, F32)
    wait_all(copies)
    totals = jnp.sum(one_hot_rows(req_ref, hot_ref), axis=0, keepdims=True)
    for d in range(wide_count):
        out_ref[d, 0:1, :] = totals
    for b in range(BLK):
        target, request = target_ref[b], req_ref[b]
        slot, rank = used_ref[target], seen_ref[request]
        used_ref[target] = slot + 1
        seen_ref[request] = rank + 1
        place_ref[b] = target * META + slot * (2 * BLK)
        out_ref[target, pl.ds(slot + 1, 1), :] = hot_ref[b : b + 1, :]
        out_ref[target, pl.ds(slot + 3, 1), :] = jnp.full((1, HD), rank, jnp.int32).astype(F32)


def describe(req, target, wide_count):
    return pl.pallas_call(
        meta_kernel,
        in_specs=[HBM, HBM],
        out_specs=[VMEM, SMEM],
        out_shape=[
            jax.ShapeDtypeStruct((wide_count, 8, HD), F32),
            jax.ShapeDtypeStruct((BLK,), jnp.int32),
        ],
        scratch_shapes=[
            pltpu.SMEM((BLK,), jnp.int32),
            pltpu.SMEM((BLK,), jnp.int32),
            pltpu.VMEM((BLK, HD), F32),
            pltpu.SMEM((wide_count,), jnp.int32),
            pltpu.SMEM((wide_count,), jnp.int32),
            pltpu.SemaphoreType.DMA((2,)),
        ],
        compiler_params=params(),
        name="describe",
    )(*stay(req, target))


def begin_kernel(me_ref, part_hbm, after_ref, row_ref, rows_ref, sems):
    me = me_ref[0]
    wait_all(start_all([(tile_of_rows(part_hbm.at[0], me, part_hbm.shape[2]), rows_ref)], sems))
    row_ref[...] = rows_ref[pl.ds(me % 8, 1), :].astype(BF16)


def begin(me, partials, after):
    depth = partials.shape[3]
    return pl.pallas_call(
        begin_kernel,
        in_specs=[SMEM, HBM, SMEM],
        out_specs=VMEM,
        out_shape=jax.ShapeDtypeStruct((1, depth), BF16),
        scratch_shapes=[pltpu.VMEM((8, depth), F32), pltpu.SemaphoreType.DMA((1,))],
        compiler_params=params(),
        name="begin",
    )(me, *stay(partials), after)


META = CAP * 2 * BLK


def project_kernel(
    x_hbm, gain_hbm, wk_hbm, wv_hbm, kgain_hbm, place_ref, after_ref,
    k_ref, v_ref, w_ref, going_hbm,
    x_ref, gain_ref, wk_ref, wv_ref, kgain_ref, going_ref, sems,
):
    count, depth = x_ref.shape
    tile, chunk = 256, depth // 4
    small = start_all([(gain_hbm, gain_ref), (kgain_hbm, kgain_ref)], sems)
    pieces = [
        pltpu.make_async_copy(x_hbm.at[pl.ds(at, tile)], x_ref.at[pl.ds(at, tile)], sems.at[4 + i])
        for i, at in enumerate(range(0, count, tile))
    ]
    weights = [
        pltpu.make_async_copy(src.at[pl.ds(at, chunk)], dst.at[pl.ds(at, chunk)], sems.at[8 + i])
        for i, (at, src, dst) in enumerate(
            (at, src, dst)
            for at in range(0, depth, chunk)
            for src, dst in ((wk_hbm, wk_ref), (wv_hbm, wv_ref))
        )
    ]
    for copy in weights:
        copy.start()
    pieces[0].start()

    going_ref[...] = jnp.zeros(going_ref.shape, BF16)
    wait_all(small)
    parts = depth // HD

    def scale(i):
        squares = jnp.zeros((tile, HD), F32)
        for p in range(0, parts, 2):
            a, b = [x_ref[i * tile : (i + 1) * tile, q * HD : (q + 1) * HD] for q in (p, p + 1)]
            squares = squares + (a * a + b * b).astype(F32)
        mean = jnp.sum(squares, axis=1, keepdims=True) * (1.0 / depth)
        return lax.rsqrt(mean + EPS)

    gain = jnp.concatenate([gain_ref[...], jnp.zeros((HD - parts, HD), F32)], axis=0).T
    for i in range(4):
        wait_all(weights[2 * i : 2 * i + 2])
        if i == 3:
            pieces[1].start()
        for p in range(i * parts // 4, (i + 1) * parts // 4):
            rows = slice(p * HD, (p + 1) * HD)
            g = gain[:, p : p + 1]
            w_ref[rows, :HD] = (wk_ref[rows, :].astype(F32) * g).astype(BF16)
            w_ref[rows, HD:] = (wv_ref[rows, :].astype(F32) * g).astype(BF16)
    pieces[0].wait()
    pieces[2].start()
    scales = scale(0)
    for i in range(len(pieces)):
        rows = slice(i * tile, (i + 1) * tile)
        if i + 1 < len(pieces):
            pieces[i + 1].wait()
            if i + 3 < len(pieces):
                pieces[i + 3].start()
        out = dot(x_ref[rows, :], w_ref[...]) * scales
        if i + 1 < len(pieces):
            scales = scale(i + 1)
        k, v = head_norm(out[:, :HD], kgain_ref[...]), out[:, HD:].astype(BF16)
        k_ref[rows, :] = k
        v_ref[rows, :] = v
        k = k.astype(BF16)
        for b in range(tile // BLK):
            part = slice(b * BLK, (b + 1) * BLK)
            both = jnp.concatenate([k[part], v[part]], axis=0)
            place = pl.multiple_of(place_ref[i * (tile // BLK) + b], 2 * BLK)
            going_ref[pl.ds(place, 2 * BLK), :] = both
    out = pltpu.make_async_copy(going_ref, going_hbm, sems.at[16])
    out.start()
    out.wait()


def project(rows, gain, wk, wv, kgain, place, after, wide_count):
    count, depth = rows.shape
    return pl.pallas_call(
        project_kernel,
        in_specs=[HBM] * 5 + [SMEM, VMEM],
        out_specs=[VMEM] * 3 + [HBM],
        out_shape=[
            jax.ShapeDtypeStruct((count, HD), F32),
            jax.ShapeDtypeStruct((count, HD), BF16),
            jax.ShapeDtypeStruct((depth, 2 * HD), BF16),
            pltpu.HBM((wide_count * META, HD), BF16),
        ],
        scratch_shapes=[
            pltpu.VMEM((count, depth), BF16),
            pltpu.VMEM((depth // HD, HD), F32),
            pltpu.VMEM((depth, HD), BF16),
            pltpu.VMEM((depth, HD), BF16),
            pltpu.VMEM((1, HD), F32),
            pltpu.VMEM((wide_count * META, HD), BF16),
            pltpu.SemaphoreType.DMA((17,)),
        ],
        compiler_params=params(28),
        cost_estimate=pl.CostEstimate(
            flops=4 * count * depth * HD, bytes_accessed=2 * count * depth, transcendentals=0
        ),
        name="project",
    )(*stay(rows, gain.reshape(depth // HD, HD), wk, wv, kgain), place, after)


def hold_kernel(*refs):
    pass


def hold(going, *after):
    return pl.pallas_call(
        hold_kernel,
        in_specs=[HBM] + [VMEM] * len(after),
        out_specs=HBM,
        out_shape=pltpu.HBM(going.shape, going.dtype),
        input_output_aliases={0: 0},
        compiler_params=params(),
        name="hold",
    )(*stay(going), *after)


def token_kernel(me_ref, a_ref, b_ref, c_ref, d_ref, res_hbm, w_ref, kgain_hbm, out_ref, res_ref, kgain_ref, sems):
    me = me_ref[0]
    copies = start_all(
        [(tile_of_rows(res_hbm, me, res_hbm.shape[1]), res_ref), (kgain_hbm, kgain_ref)], sems
    )
    added = tree([ref[...].astype(F32) for ref in (a_ref, b_ref, c_ref, d_ref)], jnp.add)
    wait_all(copies)
    hidden = res_ref[pl.ds(me % 8, 1), :] + added
    normed = hidden * lax.rsqrt(jnp.mean(hidden * hidden, axis=-1, keepdims=True) + EPS)
    wide = jnp.broadcast_to(normed, (16, normed.shape[1])).astype(BF16)
    out = dot(wide, w_ref[...])
    k, v = head_norm(out[:, :HD], kgain_ref[...]), out[:, HD:]
    out_ref[...] = jnp.where(iota(k.shape, 0) % 2 == 0, k, v)


def token(me, parts, res, w, kgain):
    return pl.pallas_call(
        token_kernel,
        in_specs=[SMEM] + [VMEM] * 4 + [HBM, VMEM, HBM],
        out_specs=VMEM,
        out_shape=jax.ShapeDtypeStruct((16, HD), F32),
        scratch_shapes=[
            pltpu.VMEM((8, res.shape[2]), F32),
            pltpu.VMEM((1, HD), F32),
            pltpu.SemaphoreType.DMA((2,)),
        ],
        compiler_params=params(),
        cost_estimate=pl.CostEstimate(
            flops=50_000_000, bytes_accessed=3_000_000, transcendentals=0
        ),
        name="token",
    )(me, *parts, *stay(res), w, *stay(kgain))


def payload_rows(tokens):
    return STAT + -(-(6 + 2 * tokens) // 16) * 16


def put_stats(ref, c, total, tok):
    hi = total.astype(BF16).astype(F32)
    pad = ref.shape[0] - STAT - 6 - tok.shape[0]
    pieces = [c, hi, total - hi, tok] + ([jnp.zeros((pad, HD), F32)] if pad else [])
    ref[STAT:, :] = jnp.concatenate(pieces, axis=0).astype(BF16)


def frequencies():
    lane = iota((1, HD), 1) % (HD // 2)
    freq = jnp.zeros((1, HD), F32)
    for i in range(HD // 2):
        freq = jnp.where(lane == i, float(np.float32(THETA ** (-2.0 * i / HD))), freq)
    return freq


def context_row(ctx_ref):
    lane = iota((1, HD), 1)
    ctx = jnp.zeros((1, HD), F32)
    for r in range(ctx_ref.shape[0]):
        ctx = jnp.where(lane == r, ctx_ref[r].astype(F32), ctx)
    return ctx


def below(size):
    return jnp.where(iota((size, size), 1) < iota((size, size), 0), 1.0, 0.0).astype(BF16)


def turns(start, sign):
    freq = frequencies()
    ang = start * freq
    cb, sb = jnp.cos(ang), jnp.sin(ang)
    ang = iota((BLK, HD), 0).astype(F32) * freq
    ct, st = jnp.cos(ang), jnp.sin(ang)

    def turned(k, b):
        c1, s1 = cb[b : b + 1], sb[b : b + 1]
        c = c1 * ct - s1 * st
        s = (s1 * ct + c1 * st) * sign
        return (k * c + pltpu.roll(k, HD // 2, 1) * s).astype(BF16)

    return turned


def attend_kernel(
    me_ref, req_hbm, ctx_hbm, q_hbm, qgain_hbm, cache_hbm, meta_ref, k_ref, v_ref, tok_ref,
    out_ref, qr_ref,
    req_ref, ctx_ref, q_ref, qgain_ref, cache_ref, hot_ref, ang_ref, kr_ref,
    q_scr, s_scr, o_scr, sems,
):
    me = me_ref[0]
    copies = start_all(
        [
            (req_hbm, req_ref),
            (ctx_hbm, ctx_ref),
            (q_hbm, q_ref),
            (qgain_hbm, qgain_ref),
            (cache_hbm, cache_ref),
        ],
        sems,
    )
    rows, slots = cache_ref.shape[1], cache_ref.shape[2]
    pairs = q_ref.shape[0]
    heads = q_ref.shape[1] // HD
    queries = heads * pairs
    per_row = queries // rows
    score_scale = HD ** (-0.5)
    freq = frequencies()
    sign = rope_sign()
    lane = iota((1, HD), 1)
    wait_all(copies[:2])

    ctx = context_row(ctx_ref)
    counts = meta_ref[:, 0, :]
    ahead = jnp.sum(jnp.where(iota(counts.shape, 0) < me, counts, 0.0), axis=0, keepdims=True)
    last = ctx + BLK * jnp.sum(counts, axis=0, keepdims=True)
    hot = one_hot_rows(req_ref, hot_ref)
    earlier = dot(below(BLK), hot.astype(BF16))
    start = jnp.sum(hot * (ctx + BLK * (ahead + earlier)), axis=1, keepdims=True)
    turned = turns(start, sign)
    for b in range(BLK):
        part = slice(b * BLK, (b + 1) * BLK)
        kr_ref[part, :] = turned(k_ref[part, :], b)

    wait_all(copies[2:])
    last = jnp.broadcast_to(last, (HD, HD)).T[:rows]
    ang = jnp.concatenate([last, last + 1.0], axis=0) * freq
    cd, sd = jnp.cos(ang), jnp.sin(ang) * sign
    for h in range(heads):
        x = head_norm(q_ref[:, h * HD : (h + 1) * HD].astype(F32), qgain_ref[...])
        qr = (x * cd + pltpu.roll(x, HD // 2, 1) * sd).astype(BF16)
        qr_ref[h * pairs : (h + 1) * pairs, :] = qr
        q_scr[h * pairs : (h + 1) * pairs, :] = qr.astype(F32)

    ang_ref[...] = cd
    cos_row = ang_ref[pl.ds(me, 1), :]
    ang_ref[...] = sd
    sin_row = ang_ref[pl.ds(me, 1), :]
    tok = tok_ref[0:8, :]
    turned = tok * cos_row + pltpu.roll(tok, HD // 2, 1) * sin_row
    tok = jnp.where(iota(tok.shape, 0) % 2 == 0, turned, tok)

    place = me * slots + iota((per_row, slots), 1)
    for r in range(rows):
        mine = pl.ds(r, per_row, stride=rows)
        s = dot_nt(q_scr[mine, :].astype(BF16), cache_ref[0, r]) * score_scale
        s_scr[mine, :] = jnp.where(place < ctx_ref[r], s, MASKED)
    owners = []
    for j in range(0, BLK, 4):
        own = jnp.where(lane < BLK, req_ref[j], req_ref[j + 1])
        own = jnp.where(lane < 2 * BLK, own, jnp.where(lane < 3 * BLK, req_ref[j + 2], req_ref[j + 3]))
        owners.append(own)
    owner = jnp.concatenate(owners, axis=1)
    block = dot_nt(qr_ref[...], kr_ref[...]) * score_scale
    block = jnp.where(iota((queries, 1), 0) % rows == owner, block, MASKED)
    cache = s_scr[...]
    top = jnp.maximum(
        jnp.max(cache, axis=1, keepdims=True), jnp.max(block, axis=1, keepdims=True)
    )
    c = jnp.maximum(top, FLOOR).astype(BF16).astype(F32)
    cache = jnp.exp(cache - c)
    block = jnp.exp(block - c)
    total = jnp.sum(cache, axis=1, keepdims=True) + jnp.sum(block, axis=1, keepdims=True)
    s_scr[...] = cache
    for r in range(rows):
        mine = pl.ds(r, per_row, stride=rows)
        o_scr[mine, :] = dot(s_scr[mine, :].astype(BF16), cache_ref[1, r])
    out_ref[:STAT, :] = (dot(block.astype(BF16), v_ref[...]) + o_scr[...]).astype(BF16)
    lane = iota((queries, HD), 1)
    both = jnp.where(lane == 0, c, jnp.where(lane == 1, total, 0.0))
    t0, t1 = both[:HD].T, both[HD:].T
    put_stats(
        out_ref,
        jnp.concatenate([t0[0:1], t1[0:1]], axis=0),
        jnp.concatenate([t0[1:2], t1[1:2]], axis=0),
        tok[0:2, :],
    )


def attend(me, req, ctx, q, qgain, cache, meta, keys, values, tok):
    return pl.pallas_call(
        attend_kernel,
        in_specs=[SMEM] + [HBM] * 5 + [VMEM] * 4,
        out_specs=[VMEM, VMEM],
        out_shape=[
            jax.ShapeDtypeStruct((payload_rows(1), HD), BF16),
            jax.ShapeDtypeStruct((STAT, HD), BF16),
        ],
        scratch_shapes=[
            pltpu.SMEM(req.shape, jnp.int32),
            pltpu.SMEM(ctx.shape, jnp.int32),
            pltpu.VMEM(q.shape, BF16),
            pltpu.VMEM(qgain.shape, F32),
            pltpu.VMEM(cache.shape, BF16),
            pltpu.VMEM((BLK, HD), F32),
            pltpu.VMEM((2 * ctx.shape[0], HD), F32),
            pltpu.VMEM(keys.shape, BF16),
        ]
        + [pltpu.VMEM((STAT, HD), F32)] * 3
        + [pltpu.SemaphoreType.DMA((5,))],
        compiler_params=params(),
        cost_estimate=pl.CostEstimate(
            flops=400_000_000, bytes_accessed=5_000_000, transcendentals=300_000
        ),
        name="attend",
    )(me, *stay(req, ctx, q, qgain, cache), meta, keys, values, tok)


def finish_kernel(ctx_hbm, came_hbm, meta_ref, after_ref, out_hbm, token_ref, ctx_ref, came_ref, out_ref, sems):
    wait_all(start_all([(ctx_hbm, ctx_ref), (came_hbm, came_ref)], sems))
    groups = came_ref.shape[0]
    counts = meta_ref[:, 0, :]
    base = context_row(ctx_ref) + BLK * dot(below(groups), counts.astype(BF16))
    sign = rope_sign()
    turned = [
        turns(
            jnp.sum(
                meta_ref[:, 1 + slot, :] * (base + BLK * meta_ref[:, 3 + slot, :]), axis=1, keepdims=True
            ),
            sign,
        )
        for slot in range(CAP)
    ]
    pr, pc = iota((2 * BLK, 2 * BLK), 0), iota((2 * BLK, 2 * BLK), 1)
    perm = jnp.where(pc == pr // 2 + BLK * (pr % 2), 1.0, 0.0).astype(BF16)
    for g in range(groups):
        for slot in range(CAP):
            at = slot * 2 * BLK
            k = turned[slot](came_ref[g, at : at + BLK, :].astype(F32), g)
            both = jnp.concatenate([k, came_ref[g, at + BLK : at + 2 * BLK, :]], axis=0)
            to = (g * CAP + slot) * 2 * BLK
            out_ref[to : to + 2 * BLK, :] = dot(perm, both).astype(BF16)
    token_ref[...] = base[:8]
    out = pltpu.make_async_copy(out_ref, out_hbm, sems.at[2])
    out.start()
    out.wait()


def finish(ctx, came, meta, after):
    shape = (came.shape[0] * META, HD)
    return pl.pallas_call(
        finish_kernel,
        in_specs=[HBM, HBM, VMEM, VMEM],
        out_specs=[HBM, VMEM],
        out_shape=[pltpu.HBM(shape, BF16), jax.ShapeDtypeStruct((8, HD), F32)],
        scratch_shapes=[
            pltpu.SMEM(ctx.shape, jnp.int32),
            pltpu.VMEM(came.shape, BF16),
            pltpu.VMEM(shape, BF16),
            pltpu.SemaphoreType.DMA((3,)),
        ],
        compiler_params=params(),
        cost_estimate=pl.CostEstimate(
            flops=80_000_000, bytes_accessed=3_000_000, transcendentals=0
        ),
        name="finish",
    )(*stay(ctx, came), meta, after)


def tree(values, op):
    while len(values) > 1:
        values = [op(values[i], values[i + 1]) for i in range(0, len(values), 2)]
    return values[0]


def merged(refs, tokens):
    add = lambda a, b: a + b
    stats = [ref[STAT:, :].astype(F32) for ref in refs]
    cs = [s[0:2] for s in stats]
    top = tree(cs, jnp.maximum)
    factors = [jnp.exp(c - top) for c in cs]
    total = tree([f * (s[2:4] + s[4:6]) for s, f in zip(stats, factors)], add)
    cols = jnp.concatenate(factors + [jnp.zeros((HD - 2 * len(refs), HD), F32)], axis=0).T
    halves = []
    for g in range(2):
        terms = [
            ref[g * HD : (g + 1) * HD, :].astype(F32) * cols[:, 2 * i + g : 2 * i + g + 1]
            for i, ref in enumerate(refs)
        ]
        halves.append(tree(terms, add))
    tok = jnp.concatenate([s[6 : 6 + 2 * tokens] for s in stats], axis=0)
    return halves, top, total, tok


def merge_kernel(*refs, tokens):
    out_ref = refs[-1]
    halves, top, total, tok = merged(refs[:-1], tokens)
    for g in range(2):
        out_ref[g * HD : (g + 1) * HD, :] = halves[g].astype(BF16)
    put_stats(out_ref, top, total, tok)


def merge(parts, tokens):
    return pl.pallas_call(
        functools.partial(merge_kernel, tokens=tokens),
        in_specs=[VMEM] * len(parts),
        out_specs=VMEM,
        out_shape=jax.ShapeDtypeStruct((payload_rows(len(parts) * tokens), HD), BF16),
        compiler_params=params(),
        name="merge",
    )(*parts)


def slot_token(slot, me):
    return me ^ (slot & 3) ^ (((slot >> 2) & 3) * 8) ^ ((slot >> 4) * 4)


def final_kernel(me_ref, qr_ref, after_ref, *refs):
    out_ref, tok_out_ref = refs[-2:]
    me = me_ref[0]
    halves, top, total, tok = merged(refs[:-2], 16)
    keys = tok.astype(BF16)
    shape = (64, 64)
    to, of = iota(shape, 0), iota(shape, 1)
    moves = (to % 2 == of % 2) & (to // 2 == slot_token(of // 2, me))
    tok_out_ref[...] = dot(jnp.where(moves, 1.0, 0.0).astype(BF16), keys).astype(BF16)
    vals = pltpu.roll(tok, 63, 0).astype(BF16)
    cols = jnp.concatenate([top, total, jnp.zeros((HD - 4, HD), F32)], axis=0).T
    row, col = iota((HD, 64), 0), iota((HD, 64), 1)
    held = slot_token(col // 2, me)
    same = (col % 2 == 0) & (held % 16 == row % 16) & (held // 16 <= (row // 16) % 2)
    for g in range(2):
        s = dot_nt(qr_ref[g * HD : (g + 1) * HD, :], keys) * (HD ** (-0.5))
        s = jnp.where(same, s, MASKED)
        c, old = cols[:, g : g + 1], cols[:, 2 + g : 3 + g]
        m = jnp.maximum(c, jnp.max(s, axis=1, keepdims=True))
        f = jnp.exp(c - m)
        p = jnp.exp(s - m)
        whole = old * f + jnp.sum(p, axis=1, keepdims=True)
        o = ((halves[g] * f + dot(p.astype(BF16), vals)) / whole).astype(BF16)
        for h in range(4):
            head = g * 4 + h
            out_ref[:, head * HD : (head + 1) * HD] = o[h * 32 : (h + 1) * 32]


def final(me, qr, after, parts):
    return pl.pallas_call(
        final_kernel,
        in_specs=[SMEM] + [VMEM] * (2 + len(parts)),
        out_specs=[VMEM, VMEM],
        out_shape=[
            jax.ShapeDtypeStruct((32, 8 * HD), BF16),
            jax.ShapeDtypeStruct((64, HD), BF16),
        ],
        compiler_params=params(),
        name="final",
    )(me, qr, after, *parts)


def exchange(value, axis, step):
    size = lax.axis_size(axis)
    return lax.ppermute(value, axis, [(i, i ^ step) for i in range(size)])


def all_to_all(value):
    return lax.all_to_all(value, "wide", split_axis=0, concat_axis=0, tiled=True)


def local(
    prefill_rows,
    in_gain,
    key_weight,
    value_weight,
    key_gain,
    query_gain,
    block_request,
    block_target,
    context_lengths,
    kv_cache,
    decode_queries,
    decode_partials,
    decode_residual,
):
    me = lax.axis_index("wide").astype(jnp.int32).reshape(1)
    wide_count = lax.axis_size("wide")
    row_count = context_lengths.shape[0]
    kgain = key_gain.reshape(1, HD)

    meta, place = describe(block_request, block_target.reshape(-1), wide_count)
    meta = all_to_all(meta)

    part = begin(me, decode_partials, place)
    other = exchange(part, "kvh", 1)
    part = (part.astype(F32) + other.astype(F32)).astype(BF16)
    decode_parts = [part] + [exchange(part, "kvh", step) for step in (2, 4, 6)]

    keys, values, weight, going = project(
        prefill_rows, in_gain, key_weight, value_weight, kgain, place, part, wide_count,
    )
    going = hold(going, *decode_parts)
    came = all_to_all(going.reshape(wide_count, META, HD))
    tok = token(me, decode_parts, decode_residual, weight, kgain)
    payload, queries = attend(
        me, block_request, context_lengths, decode_queries.reshape(2 * row_count, -1),
        query_gain.reshape(1, HD), kv_cache, meta, keys, values, tok,
    )
    parts = [payload] + [exchange(payload, "wide", step) for step in STAGES[0]]
    payload = merge(parts, 1)
    parts = [payload] + [exchange(payload, "wide", step) for step in STAGES[1]]
    payload = merge(parts, 4)
    parts = [payload] + [exchange(payload, "wide", step) for step in STAGES[2]]
    new_blocks, done = finish(context_lengths, came, meta, payload)
    attended, new = final(me, queries, done, parts)
    return (
        attended.reshape(2, row_count, -1),
        new_blocks.reshape(wide_count * CAP, BLK, 2, HD),
        new.reshape(2, row_count, 2, HD),
    )


def solution(mesh):
    placed = (
        P("wide", None),
        P(),
        P(None, "kvh"),
        P(None, "kvh"),
        P(),
        P(),
        P("wide"),
        P("wide", None),
        P(),
        P(None, None, "wide", "kvh"),
        P(None, None, "kvh"),
        P("kvh", None, None, None),
        P(),
    )
    return jax.shard_map(
        local,
        mesh=mesh,
        in_specs=placed,
        out_specs=(P(None, None, "kvh"), P("wide", None, None, "kvh"), P(None, None, None, "kvh")),
        check_vma=False,
    )
```

```python
import functools

import jax
import jax.numpy as jnp
import numpy as np
from jax import lax
from jax.experimental import pallas as pl
from jax.experimental.pallas import tpu as pltpu
from jax.sharding import PartitionSpec as P

CAP = 2
EPS = 1e-06
THETA = 1000000.0
MASKED = -3e38
FLOOR = -1e30
F32 = jnp.float32
BF16 = jnp.bfloat16

HD = 128
BLK = 32
STAT = 256
STAGES = ((1, 2, 3), (8, 16, 24), (4,))


def params(limit=16):
    return pltpu.CompilerParams(vmem_limit_bytes=limit * 1024 * 1024)


VMEM = pl.BlockSpec(memory_space=pltpu.VMEM)
SMEM = pl.BlockSpec(memory_space=pltpu.SMEM)
HBM = pl.BlockSpec(memory_space=pltpu.HBM)


def dot(a, b):
    return jnp.dot(a, b, preferred_element_type=F32)


def dot_nt(a, b):
    return lax.dot_general(a, b, (((1,), (1,)), ((), ())), preferred_element_type=F32)


def iota(shape, axis):
    return lax.broadcasted_iota(jnp.int32, shape, axis)


def rope_sign():
    return jnp.where(iota((1, HD), 1) < HD // 2, -1.0, 1.0).astype(F32)


def head_norm(x, gain):
    return x * lax.rsqrt(jnp.mean(x * x, axis=-1, keepdims=True) + EPS) * gain


def one_hot_rows(req_ref, scr):
    lane = iota((1, HD), 1)
    for b in range(BLK):
        scr[b : b + 1, :] = jnp.where(lane == req_ref[b], 1.0, 0.0)
    return scr[...]


def stay(*arrays):
    return [pltpu.with_memory_space_constraint(x, pltpu.HBM) for x in arrays]


def start_all(pairs, sems):
    copies = [pltpu.make_async_copy(src, dst, sems.at[i]) for i, (src, dst) in enumerate(pairs)]
    for copy in copies:
        copy.start()
    return copies


def wait_all(copies):
    for copy in copies:
        copy.wait()


def tile_of_rows(ref, me, rows):
    return ref.at[me // rows, pl.ds(pl.multiple_of(me % rows // 8 * 8, 8), 8), :]


def meta_kernel(
    me_ref, req_hbm, target_hbm, part_hbm, out_ref, place_ref, slots_hbm, row_ref,
    req_ref, target_ref, hot_ref, used_ref, seen_ref, zero_ref, rows_ref, sems,
):
    me = me_ref[0]
    own_rows = tile_of_rows(part_hbm.at[0], me, part_hbm.shape[2])
    zero_ref[...] = jnp.zeros(zero_ref.shape, BF16)
    size = zero_ref.shape[0]
    fills = [
        pltpu.make_async_copy(zero_ref, slots_hbm.at[pl.ds(i * size, size)], sems.at[3 + i])
        for i in range(slots_hbm.shape[0] // size)
    ]
    copies = start_all([(req_hbm, req_ref), (target_hbm, target_ref), (own_rows, rows_ref)], sems)
    for fill in fills:
        fill.start()
    wide_count = out_ref.shape[0]
    for d in range(wide_count):
        used_ref[d] = 0
        seen_ref[d] = 0
    out_ref[...] = jnp.zeros(out_ref.shape, F32)
    wait_all(copies[:2])
    totals = jnp.sum(one_hot_rows(req_ref, hot_ref), axis=0, keepdims=True)
    for d in range(wide_count):
        out_ref[d, 0:1, :] = totals
    for b in range(BLK):
        target, request = target_ref[b], req_ref[b]
        slot, rank = used_ref[target], seen_ref[request]
        used_ref[target] = slot + 1
        seen_ref[request] = rank + 1
        place_ref[b] = target * META + slot * (2 * BLK)
        out_ref[target, pl.ds(slot + 1, 1), :] = hot_ref[b : b + 1, :]
        out_ref[target, pl.ds(slot + 3, 1), :] = jnp.full((1, HD), rank, jnp.int32).astype(F32)
    copies[2].wait()
    row_ref[...] = rows_ref[pl.ds(me % 8, 1), :].astype(BF16)
    wait_all(fills)


def describe(me, req, target, partials, wide_count):
    depth = partials.shape[3]
    return pl.pallas_call(
        meta_kernel,
        in_specs=[SMEM, HBM, HBM, HBM],
        out_specs=[VMEM, SMEM, HBM, VMEM],
        out_shape=[
            jax.ShapeDtypeStruct((wide_count, 8, HD), F32),
            jax.ShapeDtypeStruct((BLK,), jnp.int32),
            pltpu.HBM((wide_count * META, HD), BF16),
            jax.ShapeDtypeStruct((1, depth), BF16),
        ],
        scratch_shapes=[
            pltpu.SMEM((BLK,), jnp.int32),
            pltpu.SMEM((BLK,), jnp.int32),
            pltpu.VMEM((BLK, HD), F32),
            pltpu.SMEM((wide_count,), jnp.int32),
            pltpu.SMEM((wide_count,), jnp.int32),
            pltpu.VMEM((1024, HD), BF16),
            pltpu.VMEM((8, depth), F32),
            pltpu.SemaphoreType.DMA((3 + wide_count * META // 1024,)),
        ],
        compiler_params=params(),
        name="describe",
    )(me, *stay(req, target, partials))


META = CAP * 2 * BLK


def project_kernel(
    x_hbm, gain_hbm, wk_hbm, wv_hbm, kgain_hbm, place_ref, after_ref, slots_hbm, w_ref, going_hbm,
    x_ref, gain_ref, wk_ref, wv_ref, kgain_ref, block_ref, sems,
):
    count, depth = x_ref.shape
    tile, chunk, parts = 256, 512, depth // HD
    tiles, load, blocks = count // tile, 1024, tile // BLK
    given = []

    def copy(src, dst):
        given.append(0)
        return pltpu.make_async_copy(src, dst, sems.at[len(given) - 1])

    xs = []
    for i in range(tiles):
        step = tile // (4, 2, 1, 1)[min(i, 3)]
        xs.append(
            [
                copy(x_hbm.at[pl.ds(at, step)], x_ref.at[pl.ds(at, step)])
                for at in range(i * tile, (i + 1) * tile, step)
            ]
        )
    weights = [
        [
            copy(src.at[pl.ds(at, load)], dst.at[pl.ds(at, load)])
            for src, dst in ((wk_hbm, wk_ref), (wv_hbm, wv_ref))
        ]
        for at in range(0, depth, load)
    ]
    small = [copy(gain_hbm, gain_ref), copy(kgain_hbm, kgain_ref)]
    outs = []
    for c in small + xs[0] + sum(weights, []) + xs[1]:
        c.start()
    wait_all(small)
    gain = jnp.concatenate([gain_ref[...], jnp.zeros((HD - parts, HD), F32)], axis=0).T
    wait_all(xs[0])

    def put(i, acc, squares):
        mean = jnp.sum(squares, axis=1, keepdims=True) * (1.0 / depth)
        full = acc * lax.rsqrt(mean + EPS)
        k, v = head_norm(full[:, :HD], kgain_ref[...]).astype(BF16), full[:, HD:].astype(BF16)
        for b in range(blocks):
            part, own = slice(b * BLK, (b + 1) * BLK), i * blocks + b
            block_ref[own] = jnp.concatenate([k[part], v[part]], axis=0)
        for own in range(i * blocks, (i + 1) * blocks):
            place = pl.multiple_of(place_ref[own], 2 * BLK)
            outs.append(copy(block_ref.at[own], going_hbm.at[pl.ds(place, 2 * BLK)]))
            outs[-1].start()

    for i in range(tiles):
        rows = slice(i * tile, (i + 1) * tile)
        if i + 2 < tiles:
            for c in xs[i + 2]:
                c.start()
        acc = jnp.zeros((tile, 2 * HD), F32)
        squares = jnp.zeros((tile, HD), F32)
        for at in range(0, depth, chunk):
            if i == 0:
                if at % load == 0:
                    wait_all(weights[at // load])
                for p in range(at // HD, (at + chunk) // HD):
                    part = slice(p * HD, (p + 1) * HD)
                    g = gain[:, p : p + 1]
                    w_ref[part, :HD] = (wk_ref[part, :].astype(F32) * g).astype(BF16)
                    w_ref[part, HD:] = (wv_ref[part, :].astype(F32) * g).astype(BF16)
            x = x_ref[rows, at : at + chunk]
            xf = x.astype(F32)
            sq = xf * xf
            for p in range(0, chunk, HD):
                squares = squares + sq[:, p : p + HD]
            acc = acc + dot(x, w_ref[at : at + chunk, :])
        if i > 0:
            put(i - 1, *held)
        held = acc, squares
        if i + 1 < tiles:
            wait_all(xs[i + 1])
    put(tiles - 1, *held)
    wait_all(outs)


def project(rows, gain, wk, wv, kgain, place, after, slots):
    count, depth = rows.shape
    return pl.pallas_call(
        project_kernel,
        in_specs=[HBM] * 5 + [SMEM, VMEM, HBM],
        out_specs=[VMEM, HBM],
        out_shape=[
            jax.ShapeDtypeStruct((depth, 2 * HD), BF16),
            pltpu.HBM(slots.shape, BF16),
        ],
        input_output_aliases={7: 1},
        scratch_shapes=[
            pltpu.VMEM((count, depth), BF16),
            pltpu.VMEM((depth // HD, HD), F32),
            pltpu.VMEM((depth, HD), BF16),
            pltpu.VMEM((depth, HD), BF16),
            pltpu.VMEM((1, HD), F32),
            pltpu.VMEM((count // BLK, 2 * BLK, HD), BF16),
            pltpu.SemaphoreType.DMA((52,)),
        ],
        compiler_params=params(28),
        cost_estimate=pl.CostEstimate(
            flops=4 * count * depth * HD, bytes_accessed=2 * count * depth, transcendentals=0
        ),
        name="project",
    )(*stay(rows, gain.reshape(depth // HD, HD), wk, wv, kgain), place, after, *stay(slots))


def hold_kernel(*refs):
    pass


def hold(going, *after):
    return pl.pallas_call(
        hold_kernel,
        in_specs=[HBM] + [VMEM] * len(after),
        out_specs=HBM,
        out_shape=pltpu.HBM(going.shape, going.dtype),
        input_output_aliases={0: 0},
        compiler_params=params(),
        name="hold",
    )(*stay(going), *after)


def token(parts, res, w, kgain):
    hidden = res + tree(parts, jnp.add)
    normed = hidden * lax.rsqrt(jnp.mean(hidden * hidden, axis=-1, keepdims=True) + EPS)
    wide = jnp.broadcast_to(normed, (16, normed.shape[1])).astype(BF16)
    out = dot(wide, w)
    k, v = head_norm(out[:, :HD], kgain), out[:, HD:]
    return jnp.where(iota(k.shape, 0) % 2 == 0, k, v)[0:8]


def payload_rows(tokens):
    return STAT + -(-(6 + 2 * tokens) // 16) * 16


def put_stats(ref, c, total, tok):
    hi = total.astype(BF16).astype(F32)
    pad = ref.shape[0] - STAT - 6 - tok.shape[0]
    pieces = [c, hi, total - hi, tok] + ([jnp.zeros((pad, HD), F32)] if pad else [])
    ref[STAT:, :] = jnp.concatenate(pieces, axis=0).astype(BF16)


def frequencies():
    lane = iota((1, HD), 1) % (HD // 2)
    freq = jnp.zeros((1, HD), F32)
    for i in range(HD // 2):
        freq = jnp.where(lane == i, float(np.float32(THETA ** (-2.0 * i / HD))), freq)
    return freq


def context_row(ctx_ref):
    lane = iota((1, HD), 1)
    ctx = jnp.zeros((1, HD), F32)
    for r in range(ctx_ref.shape[0]):
        ctx = jnp.where(lane == r, ctx_ref[r].astype(F32), ctx)
    return ctx


def below(size):
    return jnp.where(iota((size, size), 1) < iota((size, size), 0), 1.0, 0.0).astype(BF16)


def turns(start, sign):
    freq = frequencies()
    ang = start * freq
    cb, sb = jnp.cos(ang), jnp.sin(ang)
    ang = iota((BLK, HD), 0).astype(F32) * freq
    ct, st = jnp.cos(ang), jnp.sin(ang)

    def turned(k, b):
        c1, s1 = cb[b : b + 1], sb[b : b + 1]
        c = c1 * ct - s1 * st
        s = (s1 * ct + c1 * st) * sign
        return (k * c + pltpu.roll(k, HD // 2, 1) * s).astype(BF16)

    return turned


def attend_kernel(
    me_ref, place_ref, req_hbm, ctx_hbm, q_hbm, qgain_hbm, cache_hbm, res_hbm, kgain_hbm, going_hbm,
    meta_ref, w_ref,
    a_ref, b_ref, out_ref, qr_ref,
    req_ref, ctx_ref, q_ref, qgain_ref, cache_ref, res_ref, kgain_ref, block_ref, hot_ref, ang_ref,
    kr_ref, v_ref,
    q_scr, s_scr, o_scr, sems,
):
    me = me_ref[0]
    copies = start_all(
        [
            (req_hbm, req_ref),
            (ctx_hbm, ctx_ref),
            (going_hbm, block_ref),
            (q_hbm, q_ref),
            (qgain_hbm, qgain_ref),
            (tile_of_rows(res_hbm, me_ref[0], res_hbm.shape[1]), res_ref),
            (kgain_hbm, kgain_ref),
            (cache_hbm, cache_ref),
        ],
        sems,
    )
    rows, slots = cache_ref.shape[1], cache_ref.shape[2]
    pairs = q_ref.shape[0]
    heads = q_ref.shape[1] // HD
    queries = heads * pairs
    per_row = queries // rows
    score_scale = HD ** (-0.5)
    freq = frequencies()
    sign = rope_sign()
    lane = iota((1, HD), 1)
    wait_all(copies[:2])

    ctx = context_row(ctx_ref)
    counts = meta_ref[:, 0, :]
    ahead = jnp.sum(jnp.where(iota(counts.shape, 0) < me, counts, 0.0), axis=0, keepdims=True)
    last = ctx + BLK * jnp.sum(counts, axis=0, keepdims=True)
    hot = one_hot_rows(req_ref, hot_ref)
    earlier = dot(below(BLK), hot.astype(BF16))
    start = jnp.sum(hot * (ctx + BLK * (ahead + earlier)), axis=1, keepdims=True)
    turned = turns(start, sign)

    wait_all(copies[2:])
    last = jnp.broadcast_to(last, (HD, HD)).T[:rows]
    ang = jnp.concatenate([last, last + 1.0], axis=0) * freq
    cd, sd = jnp.cos(ang), jnp.sin(ang) * sign
    for h in range(heads):
        x = head_norm(q_ref[:, h * HD : (h + 1) * HD].astype(F32), qgain_ref[...])
        qr = (x * cd + pltpu.roll(x, HD // 2, 1) * sd).astype(BF16)
        qr_ref[h * pairs : (h + 1) * pairs, :] = qr
        q_scr[h * pairs : (h + 1) * pairs, :] = qr.astype(F32)

    ang_ref[...] = cd
    cos_row = ang_ref[pl.ds(me, 1), :]
    ang_ref[...] = sd
    sin_row = ang_ref[pl.ds(me, 1), :]
    tok = token(
        [ref[...].astype(F32) for ref in (a_ref, b_ref)],
        res_ref[pl.ds(me % 8, 1), :], w_ref[...], kgain_ref[...],
    )
    spun = tok * cos_row + pltpu.roll(tok, HD // 2, 1) * sin_row
    tok = jnp.where(iota(tok.shape, 0) % 2 == 0, spun, tok)

    place = me * slots + iota((per_row, slots), 1)
    for r in range(rows):
        mine = pl.ds(r, per_row, stride=rows)
        s = dot_nt(q_scr[mine, :].astype(BF16), cache_ref[0, r]) * score_scale
        s_scr[mine, :] = jnp.where(place < ctx_ref[r], s, MASKED)
    for b in range(BLK):
        part = slice(b * BLK, (b + 1) * BLK)
        place = pl.multiple_of(place_ref[b], 2 * BLK)
        kr_ref[part, :] = turned(block_ref[pl.ds(place, BLK), :].astype(F32), b)
        v_ref[part, :] = block_ref[pl.ds(place + BLK, BLK), :]
    owners = []
    for j in range(0, BLK, 4):
        own = jnp.where(lane < BLK, req_ref[j], req_ref[j + 1])
        own = jnp.where(lane < 2 * BLK, own, jnp.where(lane < 3 * BLK, req_ref[j + 2], req_ref[j + 3]))
        owners.append(own)
    owner = jnp.concatenate(owners, axis=1)
    block = dot_nt(qr_ref[...], kr_ref[...]) * score_scale
    block = jnp.where(iota((queries, 1), 0) % rows == owner, block, MASKED)
    cache = s_scr[...]
    top = jnp.maximum(
        jnp.max(cache, axis=1, keepdims=True), jnp.max(block, axis=1, keepdims=True)
    )
    c = jnp.maximum(top, FLOOR).astype(BF16).astype(F32)
    cache = jnp.exp(cache - c)
    block = jnp.exp(block - c)
    total = jnp.sum(cache, axis=1, keepdims=True) + jnp.sum(block, axis=1, keepdims=True)
    s_scr[...] = cache
    for r in range(rows):
        mine = pl.ds(r, per_row, stride=rows)
        o_scr[mine, :] = dot(s_scr[mine, :].astype(BF16), cache_ref[1, r])
    out_ref[:STAT, :] = (dot(block.astype(BF16), v_ref[...]) + o_scr[...]).astype(BF16)
    lane = iota((queries, HD), 1)
    both = jnp.where(lane == 0, c, jnp.where(lane == 1, total, 0.0))
    t0, t1 = both[:HD].T, both[HD:].T
    put_stats(
        out_ref,
        jnp.concatenate([t0[0:1], t1[0:1]], axis=0),
        jnp.concatenate([t0[1:2], t1[1:2]], axis=0),
        tok[0:2, :],
    )


def attend(me, place, req, ctx, q, qgain, cache, res, kgain, going, meta, weight, parts):
    return pl.pallas_call(
        attend_kernel,
        in_specs=[SMEM, SMEM] + [HBM] * 8 + [VMEM] * 4,
        out_specs=[VMEM, VMEM],
        out_shape=[
            jax.ShapeDtypeStruct((payload_rows(1), HD), BF16),
            jax.ShapeDtypeStruct((STAT, HD), BF16),
        ],
        scratch_shapes=[
            pltpu.SMEM(req.shape, jnp.int32),
            pltpu.SMEM(ctx.shape, jnp.int32),
            pltpu.VMEM(q.shape, BF16),
            pltpu.VMEM(qgain.shape, F32),
            pltpu.VMEM(cache.shape, BF16),
            pltpu.VMEM((8, res.shape[2]), F32),
            pltpu.VMEM(kgain.shape, F32),
            pltpu.VMEM(going.shape, BF16),
            pltpu.VMEM((BLK, HD), F32),
            pltpu.VMEM((2 * ctx.shape[0], HD), F32),
            pltpu.VMEM((BLK * BLK, HD), BF16),
            pltpu.VMEM((BLK * BLK, HD), BF16),
        ]
        + [pltpu.VMEM((STAT, HD), F32)] * 3
        + [pltpu.SemaphoreType.DMA((8,))],
        compiler_params=params(),
        cost_estimate=pl.CostEstimate(
            flops=400_000_000, bytes_accessed=5_000_000, transcendentals=300_000
        ),
        name="attend",
    )(me, place, *stay(req, ctx, q, qgain, cache, res, kgain, going), meta, weight, *parts)


def finish_kernel(ctx_hbm, came_hbm, meta_ref, after_ref, out_hbm, token_ref, ctx_ref, came_ref, out_ref, sems):
    groups = came_ref.shape[0]
    step = groups // 4
    size = step * META
    context = pltpu.make_async_copy(ctx_hbm, ctx_ref, sems.at[0])
    context.start()
    loads = [
        pltpu.make_async_copy(
            came_hbm.at[pl.ds(i * step, step)], came_ref.at[pl.ds(i * step, step)], sems.at[1 + i]
        )
        for i in range(4)
    ]
    stores = [
        pltpu.make_async_copy(
            out_ref.at[pl.ds(i * size, size)], out_hbm.at[pl.ds(i * size, size)], sems.at[5 + i]
        )
        for i in range(4)
    ]
    for load in loads:
        load.start()
    sign = rope_sign()
    pr, pc = iota((2 * BLK, 2 * BLK), 0), iota((2 * BLK, 2 * BLK), 1)
    perm = jnp.where(pc == pr // 2 + BLK * (pr % 2), 1.0, 0.0).astype(BF16)
    counts = meta_ref[:, 0, :]
    ahead = BLK * dot(below(groups), counts.astype(BF16))
    context.wait()
    base = context_row(ctx_ref) + ahead
    turned = [
        turns(
            jnp.sum(
                meta_ref[:, 1 + slot, :] * (base + BLK * meta_ref[:, 3 + slot, :]), axis=1, keepdims=True
            ),
            sign,
        )
        for slot in range(CAP)
    ]
    token_ref[...] = base[:8]
    for i in range(4):
        loads[i].wait()
        for g in range(i * step, (i + 1) * step):
            for slot in range(CAP):
                at = slot * 2 * BLK
                k = turned[slot](came_ref[g, at : at + BLK, :].astype(F32), g)
                both = jnp.concatenate([k, came_ref[g, at + BLK : at + 2 * BLK, :]], axis=0)
                to = (g * CAP + slot) * 2 * BLK
                out_ref[to : to + 2 * BLK, :] = dot(perm, both).astype(BF16)
        stores[i].start()
    wait_all(stores)


def finish(ctx, came, meta, after):
    shape = (came.shape[0] * META, HD)
    return pl.pallas_call(
        finish_kernel,
        in_specs=[HBM, HBM, VMEM, VMEM],
        out_specs=[HBM, VMEM],
        out_shape=[pltpu.HBM(shape, BF16), jax.ShapeDtypeStruct((8, HD), F32)],
        scratch_shapes=[
            pltpu.SMEM(ctx.shape, jnp.int32),
            pltpu.VMEM(came.shape, BF16),
            pltpu.VMEM(shape, BF16),
            pltpu.SemaphoreType.DMA((9,)),
        ],
        compiler_params=params(),
        cost_estimate=pl.CostEstimate(
            flops=80_000_000, bytes_accessed=3_000_000, transcendentals=0
        ),
        name="finish",
    )(*stay(ctx, came), meta, after)


def tree(values, op):
    while len(values) > 1:
        values = [op(values[i], values[i + 1]) for i in range(0, len(values), 2)]
    return values[0]


def merged(refs, tokens):
    add = lambda a, b: a + b
    stats = [ref[STAT:, :].astype(F32) for ref in refs]
    cs = [s[0:2] for s in stats]
    top = tree(cs, jnp.maximum)
    factors = [jnp.exp(c - top) for c in cs]
    total = tree([f * (s[2:4] + s[4:6]) for s, f in zip(stats, factors)], add)
    cols = jnp.concatenate(factors + [jnp.zeros((HD - 2 * len(refs), HD), F32)], axis=0).T
    halves = []
    for g in range(2):
        terms = [
            ref[g * HD : (g + 1) * HD, :].astype(F32) * cols[:, 2 * i + g : 2 * i + g + 1]
            for i, ref in enumerate(refs)
        ]
        halves.append(tree(terms, add))
    tok = jnp.concatenate([s[6 : 6 + 2 * tokens] for s in stats], axis=0)
    return halves, top, total, tok


def merge_kernel(*refs, tokens):
    out_ref = refs[-1]
    halves, top, total, tok = merged(refs[:-1], tokens)
    for g in range(2):
        out_ref[g * HD : (g + 1) * HD, :] = halves[g].astype(BF16)
    put_stats(out_ref, top, total, tok)


def merge(parts, tokens):
    return pl.pallas_call(
        functools.partial(merge_kernel, tokens=tokens),
        in_specs=[VMEM] * len(parts),
        out_specs=VMEM,
        out_shape=jax.ShapeDtypeStruct((payload_rows(len(parts) * tokens), HD), BF16),
        compiler_params=params(),
        name="merge",
    )(*parts)


def slot_token(slot, me):
    return me ^ (slot & 3) ^ (((slot >> 2) & 3) * 8) ^ ((slot >> 4) * 4)


def final_kernel(me_ref, qr_ref, after_ref, *refs):
    out_ref, tok_out_ref = refs[-2:]
    me = me_ref[0]
    halves, top, total, tok = merged(refs[:-2], 16)
    keys = tok.astype(BF16)
    shape = (64, 64)
    to, of = iota(shape, 0), iota(shape, 1)
    moves = (to % 2 == of % 2) & (to // 2 == slot_token(of // 2, me))
    tok_out_ref[...] = dot(jnp.where(moves, 1.0, 0.0).astype(BF16), keys).astype(BF16)
    vals = pltpu.roll(tok, 63, 0).astype(BF16)
    cols = jnp.concatenate([top, total, jnp.zeros((HD - 4, HD), F32)], axis=0).T
    row, col = iota((HD, 64), 0), iota((HD, 64), 1)
    held = slot_token(col // 2, me)
    same = (col % 2 == 0) & (held % 16 == row % 16) & (held // 16 <= (row // 16) % 2)
    for g in range(2):
        s = dot_nt(qr_ref[g * HD : (g + 1) * HD, :], keys) * (HD ** (-0.5))
        s = jnp.where(same, s, MASKED)
        c, old = cols[:, g : g + 1], cols[:, 2 + g : 3 + g]
        m = jnp.maximum(c, jnp.max(s, axis=1, keepdims=True))
        f = jnp.exp(c - m)
        p = jnp.exp(s - m)
        whole = old * f + jnp.sum(p, axis=1, keepdims=True)
        o = ((halves[g] * f + dot(p.astype(BF16), vals)) / whole).astype(BF16)
        for h in range(4):
            head = g * 4 + h
            out_ref[:, head * HD : (head + 1) * HD] = o[h * 32 : (h + 1) * 32]


def final(me, qr, after, parts):
    return pl.pallas_call(
        final_kernel,
        in_specs=[SMEM] + [VMEM] * (2 + len(parts)),
        out_specs=[VMEM, VMEM],
        out_shape=[
            jax.ShapeDtypeStruct((32, 8 * HD), BF16),
            jax.ShapeDtypeStruct((64, HD), BF16),
        ],
        compiler_params=params(),
        name="final",
    )(me, qr, after, *parts)


def exchange(value, axis, step):
    size = lax.axis_size(axis)
    return lax.ppermute(value, axis, [(i, i ^ step) for i in range(size)])


def add_bf16(a, b):
    return (a.astype(F32) + b.astype(F32)).astype(BF16)


def all_to_all(value):
    return lax.all_to_all(value, "wide", split_axis=0, concat_axis=0, tiled=True)


def local(
    prefill_rows,
    in_gain,
    key_weight,
    value_weight,
    key_gain,
    query_gain,
    block_request,
    block_target,
    context_lengths,
    kv_cache,
    decode_queries,
    decode_partials,
    decode_residual,
):
    me = lax.axis_index("wide").astype(jnp.int32).reshape(1)
    wide_count = lax.axis_size("wide")
    row_count = context_lengths.shape[0]
    kgain = key_gain.reshape(1, HD)

    meta, place, slots, part = describe(
        me, block_request, block_target.reshape(-1), decode_partials, wide_count
    )
    meta = all_to_all(meta)

    first = part = add_bf16(part, exchange(part, "kvh", 1))
    part = add_bf16(part, exchange(part, "kvh", 2))
    decode_parts = [part, exchange(part, "kvh", 4)]

    weight, going = project(
        prefill_rows, in_gain, key_weight, value_weight, kgain, place, first, slots,
    )
    going = hold(going, *decode_parts)
    came = all_to_all(going.reshape(wide_count, META, HD))
    payload, queries = attend(
        me, place, block_request, context_lengths, decode_queries.reshape(2 * row_count, -1),
        query_gain.reshape(1, HD), kv_cache,
        decode_residual, kgain, going, meta, weight, decode_parts,
    )
    parts = [payload] + [exchange(payload, "wide", step) for step in STAGES[0]]
    payload = merge(parts, 1)
    parts = [payload] + [exchange(payload, "wide", step) for step in STAGES[1]]
    payload = merge(parts, 4)
    parts = [payload] + [exchange(payload, "wide", step) for step in STAGES[2]]
    new_blocks, done = finish(context_lengths, came, meta, payload)
    attended, new = final(me, queries, done, parts)
    return (
        attended.reshape(2, row_count, -1),
        new_blocks.reshape(wide_count * CAP, BLK, 2, HD),
        new.reshape(2, row_count, 2, HD),
    )


def solution(mesh):
    placed = (
        P("wide", None),
        P(),
        P(None, "kvh"),
        P(None, "kvh"),
        P(),
        P(),
        P("wide"),
        P("wide", None),
        P(),
        P(None, None, "wide", "kvh"),
        P(None, None, "kvh"),
        P("kvh", None, None, None),
        P(),
    )
    return jax.shard_map(
        local,
        mesh=mesh,
        in_specs=placed,
        out_specs=(P(None, None, "kvh"), P("wide", None, None, "kvh"), P(None, None, None, "kvh")),
        check_vma=False,
    )
```

```python
import functools

import jax
import jax.numpy as jnp
import numpy as np
from jax import lax
from jax.experimental import pallas as pl
from jax.experimental.pallas import tpu as pltpu
from jax.sharding import PartitionSpec as P

CAP = 2
EPS = 1e-06
THETA = 1000000.0
MASKED = -3e38
FLOOR = -1e30
F32 = jnp.float32
BF16 = jnp.bfloat16

HD = 128
BLK = 32
STAT = 256
STAGES = ((1, 2, 3), (8, 16, 24), (4,))


def params(limit=16):
    return pltpu.CompilerParams(vmem_limit_bytes=limit * 1024 * 1024)


VMEM = pl.BlockSpec(memory_space=pltpu.VMEM)
SMEM = pl.BlockSpec(memory_space=pltpu.SMEM)
HBM = pl.BlockSpec(memory_space=pltpu.HBM)


def dot(a, b):
    return jnp.dot(a, b, preferred_element_type=F32)


def dot_nt(a, b):
    return lax.dot_general(a, b, (((1,), (1,)), ((), ())), preferred_element_type=F32)


def iota(shape, axis):
    return lax.broadcasted_iota(jnp.int32, shape, axis)


def rope_sign():
    return jnp.where(iota((1, HD), 1) < HD // 2, -1.0, 1.0).astype(F32)


def head_norm(x, gain):
    return x * lax.rsqrt(jnp.mean(x * x, axis=-1, keepdims=True) + EPS) * gain


def slots_of(target_ref, used_ref, place_ref):
    for d in range(used_ref.shape[0]):
        used_ref[d] = 0
    for b in range(BLK):
        target = target_ref[b]
        slot = used_ref[target]
        used_ref[target] = slot + 1
        place_ref[b] = target * META + slot * (2 * BLK)


def one_hot_rows(req_ref, scr):
    lane = iota((1, HD), 1)
    for b in range(BLK):
        scr[b : b + 1, :] = jnp.where(lane == req_ref[b], 1.0, 0.0)
    return scr[...]


def stay(*arrays):
    return [pltpu.with_memory_space_constraint(x, pltpu.HBM) for x in arrays]


def start_all(pairs, sems):
    copies = [pltpu.make_async_copy(src, dst, sems.at[i]) for i, (src, dst) in enumerate(pairs)]
    for copy in copies:
        copy.start()
    return copies


def wait_all(copies):
    for copy in copies:
        copy.wait()


def tile_of_rows(ref, me, rows):
    return ref.at[me // rows, pl.ds(pl.multiple_of(me % rows // 8 * 8, 8), 8), :]


def meta_kernel(
    req_hbm, target_hbm, part_hbm, out_ref, slots_hbm, row_ref,
    req_ref, target_ref, hot_ref, used_ref, seen_ref, zero_ref, rows_ref, sems,
):
    me = lax.axis_index("wide")
    own_rows = tile_of_rows(part_hbm.at[0], me, part_hbm.shape[2])
    zero_ref[...] = jnp.zeros(zero_ref.shape, BF16)
    size = zero_ref.shape[0]
    fills = [
        pltpu.make_async_copy(zero_ref, slots_hbm.at[pl.ds(i * size, size)], sems.at[3 + i])
        for i in range(slots_hbm.shape[0] // size)
    ]
    copies = start_all([(req_hbm, req_ref), (target_hbm, target_ref), (own_rows, rows_ref)], sems)
    for fill in fills:
        fill.start()
    wide_count = out_ref.shape[0]
    for d in range(wide_count):
        used_ref[d] = 0
        seen_ref[d] = 0
    out_ref[...] = jnp.zeros(out_ref.shape, F32)
    wait_all(copies[:2])
    totals = jnp.sum(one_hot_rows(req_ref, hot_ref), axis=0, keepdims=True)
    lane = iota((1, HD), 1)
    for d in range(wide_count):
        out_ref[d] = totals
    for b in range(BLK):
        target, request = target_ref[b], req_ref[b]
        slot, rank = used_ref[target], seen_ref[request]
        used_ref[target] = slot + 1
        seen_ref[request] = rank + 1
        row = out_ref[target]
        row = jnp.where(lane == 16 + slot, (request + 1).astype(F32), row)
        out_ref[target] = jnp.where(lane == 18 + slot, rank.astype(F32), row)
    copies[2].wait()
    row_ref[...] = rows_ref[pl.ds(me % 8, 1), :].astype(BF16)
    wait_all(fills)


def describe(req, target, partials, wide_count):
    depth = partials.shape[3]
    return pl.pallas_call(
        meta_kernel,
        in_specs=[HBM, HBM, HBM],
        out_specs=[VMEM, HBM, VMEM],
        out_shape=[
            jax.ShapeDtypeStruct((wide_count, 1, HD), F32),
            pltpu.HBM((wide_count * META, HD), BF16),
            jax.ShapeDtypeStruct((1, depth), BF16),
        ],
        scratch_shapes=[
            pltpu.SMEM((BLK,), jnp.int32),
            pltpu.SMEM((BLK,), jnp.int32),
            pltpu.VMEM((BLK, HD), F32),
            pltpu.SMEM((wide_count,), jnp.int32),
            pltpu.SMEM((wide_count,), jnp.int32),
            pltpu.VMEM((1024, HD), BF16),
            pltpu.VMEM((8, depth), F32),
            pltpu.SemaphoreType.DMA((3 + wide_count * META // 1024,)),
        ],
        compiler_params=params(),
        name="describe",
    )(*stay(req, target, partials))


META = CAP * 2 * BLK


def project_kernel(
    x_hbm, gain_hbm, wk_hbm, wv_hbm, kgain_hbm, target_hbm, after_ref, slots_hbm, w_ref, going_hbm,
    x_ref, gain_ref, wk_ref, wv_ref, kgain_ref, target_ref, used_ref, place_ref, block_ref, sems,
):
    count, depth = x_ref.shape
    tile, chunk, parts = 256, 512, depth // HD
    tiles, load, blocks = count // tile, 1024, tile // BLK
    given = []

    def copy(src, dst):
        given.append(0)
        return pltpu.make_async_copy(src, dst, sems.at[len(given) - 1])

    xs = []
    for i in range(tiles):
        step = tile // (4, 2, 1, 1)[min(i, 3)]
        xs.append(
            [
                copy(x_hbm.at[pl.ds(at, step)], x_ref.at[pl.ds(at, step)])
                for at in range(i * tile, (i + 1) * tile, step)
            ]
        )
    weights = [
        [
            copy(src.at[pl.ds(at, load)], dst.at[pl.ds(at, load)])
            for src, dst in ((wk_hbm, wk_ref), (wv_hbm, wv_ref))
        ]
        for at in range(0, depth, load)
    ]
    small = [copy(gain_hbm, gain_ref), copy(kgain_hbm, kgain_ref), copy(target_hbm, target_ref)]
    outs = []
    for c in small + xs[0] + sum(weights, []) + xs[1]:
        c.start()
    wait_all(small)
    slots_of(target_ref, used_ref, place_ref)
    gain = jnp.concatenate([gain_ref[...], jnp.zeros((HD - parts, HD), F32)], axis=0).T
    wait_all(xs[0])

    def put(i, acc, squares):
        mean = jnp.sum(squares, axis=1, keepdims=True) * (1.0 / depth)
        full = acc * lax.rsqrt(mean + EPS)
        k, v = head_norm(full[:, :HD], kgain_ref[...]).astype(BF16), full[:, HD:].astype(BF16)
        for b in range(blocks):
            part, own = slice(b * BLK, (b + 1) * BLK), i * blocks + b
            block_ref[own] = jnp.concatenate([k[part], v[part]], axis=0)
        for own in range(i * blocks, (i + 1) * blocks):
            place = pl.multiple_of(place_ref[own], 2 * BLK)
            outs.append(copy(block_ref.at[own], going_hbm.at[pl.ds(place, 2 * BLK)]))
            outs[-1].start()

    for i in range(tiles):
        rows = slice(i * tile, (i + 1) * tile)
        if i + 2 < tiles:
            for c in xs[i + 2]:
                c.start()
        acc = jnp.zeros((tile, 2 * HD), F32)
        squares = jnp.zeros((tile, HD), F32)
        for at in range(0, depth, chunk):
            if i == 0:
                if at % load == 0:
                    wait_all(weights[at // load])
                for p in range(at // HD, (at + chunk) // HD):
                    part = slice(p * HD, (p + 1) * HD)
                    g = gain[:, p : p + 1]
                    w_ref[part, :HD] = (wk_ref[part, :].astype(F32) * g).astype(BF16)
                    w_ref[part, HD:] = (wv_ref[part, :].astype(F32) * g).astype(BF16)
            x = x_ref[rows, at : at + chunk]
            xf = x.astype(F32)
            sq = xf * xf
            for p in range(0, chunk, HD):
                squares = squares + sq[:, p : p + HD]
            acc = acc + dot(x, w_ref[at : at + chunk, :])
        if i > 0:
            put(i - 1, *held)
        held = acc, squares
        if i + 1 < tiles:
            wait_all(xs[i + 1])
    put(tiles - 1, *held)
    wait_all(outs)


def project(rows, gain, wk, wv, kgain, target, after, slots, wide_count):
    count, depth = rows.shape
    return pl.pallas_call(
        project_kernel,
        in_specs=[HBM] * 6 + [VMEM, HBM],
        out_specs=[VMEM, HBM],
        out_shape=[
            jax.ShapeDtypeStruct((depth, 2 * HD), BF16),
            pltpu.HBM(slots.shape, BF16),
        ],
        input_output_aliases={7: 1},
        scratch_shapes=[
            pltpu.VMEM((count, depth), BF16),
            pltpu.VMEM((depth // HD, HD), F32),
            pltpu.VMEM((depth, HD), BF16),
            pltpu.VMEM((depth, HD), BF16),
            pltpu.VMEM((1, HD), F32),
            pltpu.SMEM(target.shape, jnp.int32),
            pltpu.SMEM((wide_count,), jnp.int32),
            pltpu.SMEM(target.shape, jnp.int32),
            pltpu.VMEM((count // BLK, 2 * BLK, HD), BF16),
            pltpu.SemaphoreType.DMA((53,)),
        ],
        compiler_params=params(28),
        cost_estimate=pl.CostEstimate(
            flops=4 * count * depth * HD, bytes_accessed=2 * count * depth, transcendentals=0
        ),
        name="project",
    )(*stay(rows, gain.reshape(depth // HD, HD), wk, wv, kgain, target), after, *stay(slots))


def hold_kernel(*refs):
    pass


def hold(going, *after):
    return pl.pallas_call(
        hold_kernel,
        in_specs=[HBM] + [VMEM] * len(after),
        out_specs=HBM,
        out_shape=pltpu.HBM(going.shape, going.dtype),
        input_output_aliases={0: 0},
        compiler_params=params(),
        name="hold",
    )(*stay(going), *after)


def token(parts, res, w, kgain):
    hidden = res + tree(parts, jnp.add)
    normed = hidden * lax.rsqrt(jnp.mean(hidden * hidden, axis=-1, keepdims=True) + EPS)
    wide = jnp.broadcast_to(normed, (16, normed.shape[1])).astype(BF16)
    out = dot(wide, w)
    k, v = head_norm(out[:, :HD], kgain), out[:, HD:]
    return jnp.where(iota(k.shape, 0) % 2 == 0, k, v)[0:8]


def payload_rows(tokens):
    return STAT + -(-(6 + 2 * tokens) // 16) * 16


def put_stats(ref, c, total, tok):
    hi = total.astype(BF16).astype(F32)
    pad = ref.shape[0] - STAT - 6 - tok.shape[0]
    pieces = [c, hi, total - hi, tok] + ([jnp.zeros((pad, HD), F32)] if pad else [])
    ref[STAT:, :] = jnp.concatenate(pieces, axis=0).astype(BF16)


def frequencies():
    lane = iota((1, HD), 1) % (HD // 2)
    freq = jnp.zeros((1, HD), F32)
    for i in range(HD // 2):
        freq = jnp.where(lane == i, float(np.float32(THETA ** (-2.0 * i / HD))), freq)
    return freq


def context_row(ctx_ref):
    lane = iota((1, HD), 1)
    ctx = jnp.zeros((1, HD), F32)
    for r in range(ctx_ref.shape[0]):
        ctx = jnp.where(lane == r, ctx_ref[r].astype(F32), ctx)
    return ctx


def below(size):
    return jnp.where(iota((size, size), 1) < iota((size, size), 0), 1.0, 0.0).astype(BF16)


def turns(start, sign):
    freq = frequencies()
    ang = start * freq
    cb, sb = jnp.cos(ang), jnp.sin(ang)
    ang = iota((BLK, HD), 0).astype(F32) * freq
    ct, st = jnp.cos(ang), jnp.sin(ang)

    def turned(k, b):
        c1, s1 = cb[b : b + 1], sb[b : b + 1]
        c = c1 * ct - s1 * st
        s = (s1 * ct + c1 * st) * sign
        return (k * c + pltpu.roll(k, HD // 2, 1) * s).astype(BF16)

    return turned


def attend_kernel(
    req_hbm, target_hbm, ctx_hbm, q_hbm, qgain_hbm, cache_hbm, res_hbm, kgain_hbm, going_hbm,
    meta_ref, w_ref,
    a_ref, b_ref, out_ref, qr_ref,
    req_ref, target_ref, ctx_ref, used_ref, place_ref, q_ref, qgain_ref, cache_ref, res_ref, kgain_ref, block_ref, hot_ref, ang_ref,
    kr_ref, v_ref,
    q_scr, s_scr, o_scr, sems,
):
    me = lax.axis_index("wide")
    copies = start_all(
        [
            (req_hbm, req_ref),
            (target_hbm, target_ref),
            (ctx_hbm, ctx_ref),
            (going_hbm, block_ref),
            (q_hbm, q_ref),
            (qgain_hbm, qgain_ref),
            (tile_of_rows(res_hbm, me, res_hbm.shape[1]), res_ref),
            (kgain_hbm, kgain_ref),
            (cache_hbm, cache_ref),
        ],
        sems,
    )
    rows, slots = cache_ref.shape[1], cache_ref.shape[2]
    pairs = q_ref.shape[0]
    heads = q_ref.shape[1] // HD
    queries = heads * pairs
    per_row = queries // rows
    score_scale = HD ** (-0.5)
    freq = frequencies()
    sign = rope_sign()
    lane = iota((1, HD), 1)
    wait_all(copies[:3])
    slots_of(target_ref, used_ref, place_ref)

    ctx = context_row(ctx_ref)
    counts = meta_ref[:, 0, :]
    counts = jnp.where(iota(counts.shape, 1) < rows, counts, 0.0)
    ahead = jnp.sum(jnp.where(iota(counts.shape, 0) < me, counts, 0.0), axis=0, keepdims=True)
    last = ctx + BLK * jnp.sum(counts, axis=0, keepdims=True)
    hot = one_hot_rows(req_ref, hot_ref)
    earlier = dot(below(BLK), hot.astype(BF16))
    start = jnp.sum(hot * (ctx + BLK * (ahead + earlier)), axis=1, keepdims=True)
    turned = turns(start, sign)

    wait_all(copies[3:])
    last = jnp.broadcast_to(last, (HD, HD)).T[:rows]
    ang = jnp.concatenate([last, last + 1.0], axis=0) * freq
    cd, sd = jnp.cos(ang), jnp.sin(ang) * sign
    for h in range(heads):
        x = head_norm(q_ref[:, h * HD : (h + 1) * HD].astype(F32), qgain_ref[...])
        qr = (x * cd + pltpu.roll(x, HD // 2, 1) * sd).astype(BF16)
        qr_ref[h * pairs : (h + 1) * pairs, :] = qr
        q_scr[h * pairs : (h + 1) * pairs, :] = qr.astype(F32)

    ang_ref[...] = cd
    cos_row = ang_ref[pl.ds(me, 1), :]
    ang_ref[...] = sd
    sin_row = ang_ref[pl.ds(me, 1), :]
    tok = token(
        [ref[...].astype(F32) for ref in (a_ref, b_ref)],
        res_ref[pl.ds(me % 8, 1), :], w_ref[...], kgain_ref[...],
    )
    spun = tok * cos_row + pltpu.roll(tok, HD // 2, 1) * sin_row
    tok = jnp.where(iota(tok.shape, 0) % 2 == 0, spun, tok)

    place = me * slots + iota((per_row, slots), 1)
    for r in range(rows):
        mine = pl.ds(r, per_row, stride=rows)
        s = dot_nt(q_scr[mine, :].astype(BF16), cache_ref[0, r]) * score_scale
        s_scr[mine, :] = jnp.where(place < ctx_ref[r], s, MASKED)
    for b in range(BLK):
        part = slice(b * BLK, (b + 1) * BLK)
        place = pl.multiple_of(place_ref[b], 2 * BLK)
        kr_ref[part, :] = turned(block_ref[pl.ds(place, BLK), :].astype(F32), b)
        v_ref[part, :] = block_ref[pl.ds(place + BLK, BLK), :]
    owners = []
    for j in range(0, BLK, 4):
        own = jnp.where(lane < BLK, req_ref[j], req_ref[j + 1])
        own = jnp.where(lane < 2 * BLK, own, jnp.where(lane < 3 * BLK, req_ref[j + 2], req_ref[j + 3]))
        owners.append(own)
    owner = jnp.concatenate(owners, axis=1)
    block = dot_nt(qr_ref[...], kr_ref[...]) * score_scale
    block = jnp.where(iota((queries, 1), 0) % rows == owner, block, MASKED)
    cache = s_scr[...]
    top = jnp.maximum(
        jnp.max(cache, axis=1, keepdims=True), jnp.max(block, axis=1, keepdims=True)
    )
    c = jnp.maximum(top, FLOOR).astype(BF16).astype(F32)
    cache = jnp.exp(cache - c)
    block = jnp.exp(block - c)
    total = jnp.sum(cache, axis=1, keepdims=True) + jnp.sum(block, axis=1, keepdims=True)
    s_scr[...] = cache
    for r in range(rows):
        mine = pl.ds(r, per_row, stride=rows)
        o_scr[mine, :] = dot(s_scr[mine, :].astype(BF16), cache_ref[1, r])
    out_ref[:STAT, :] = (dot(block.astype(BF16), v_ref[...]) + o_scr[...]).astype(BF16)
    lane = iota((queries, HD), 1)
    both = jnp.where(lane == 0, c, jnp.where(lane == 1, total, 0.0))
    t0, t1 = both[:HD].T, both[HD:].T
    put_stats(
        out_ref,
        jnp.concatenate([t0[0:1], t1[0:1]], axis=0),
        jnp.concatenate([t0[1:2], t1[1:2]], axis=0),
        tok[0:2, :],
    )


def attend(req, target, ctx, q, qgain, cache, res, kgain, going, meta, weight, parts):
    return pl.pallas_call(
        attend_kernel,
        in_specs=[HBM] * 9 + [VMEM] * 4,
        out_specs=[VMEM, VMEM],
        out_shape=[
            jax.ShapeDtypeStruct((payload_rows(1), HD), BF16),
            jax.ShapeDtypeStruct((STAT, HD), BF16),
        ],
        scratch_shapes=[
            pltpu.SMEM(req.shape, jnp.int32),
            pltpu.SMEM(target.shape, jnp.int32),
            pltpu.SMEM(ctx.shape, jnp.int32),
            pltpu.SMEM((meta.shape[0],), jnp.int32),
            pltpu.SMEM(target.shape, jnp.int32),
            pltpu.VMEM(q.shape, BF16),
            pltpu.VMEM(qgain.shape, F32),
            pltpu.VMEM(cache.shape, BF16),
            pltpu.VMEM((8, res.shape[2]), F32),
            pltpu.VMEM(kgain.shape, F32),
            pltpu.VMEM(going.shape, BF16),
            pltpu.VMEM((BLK, HD), F32),
            pltpu.VMEM((2 * ctx.shape[0], HD), F32),
            pltpu.VMEM((BLK * BLK, HD), BF16),
            pltpu.VMEM((BLK * BLK, HD), BF16),
        ]
        + [pltpu.VMEM((STAT, HD), F32)] * 3
        + [pltpu.SemaphoreType.DMA((9,))],
        compiler_params=params(),
        cost_estimate=pl.CostEstimate(
            flops=400_000_000, bytes_accessed=5_000_000, transcendentals=300_000
        ),
        name="attend",
    )(*stay(req, target, ctx, q, qgain, cache, res, kgain, going), meta, weight, *parts)


def finish_kernel(ctx_hbm, came_hbm, meta_ref, after_ref, out_hbm, token_ref, ctx_ref, came_ref, out_ref, sems):
    groups = came_ref.shape[0]
    step = groups // 4
    size = step * META
    context = pltpu.make_async_copy(ctx_hbm, ctx_ref, sems.at[0])
    context.start()
    loads = [
        pltpu.make_async_copy(
            came_hbm.at[pl.ds(i * step, step)], came_ref.at[pl.ds(i * step, step)], sems.at[1 + i]
        )
        for i in range(4)
    ]
    stores = [
        pltpu.make_async_copy(
            out_ref.at[pl.ds(i * size, size)], out_hbm.at[pl.ds(i * size, size)], sems.at[5 + i]
        )
        for i in range(4)
    ]
    for load in loads:
        load.start()
    sign = rope_sign()
    pr, pc = iota((2 * BLK, 2 * BLK), 0), iota((2 * BLK, 2 * BLK), 1)
    perm = jnp.where(pc == pr // 2 + BLK * (pr % 2), 1.0, 0.0).astype(BF16)
    facts = meta_ref[:, 0, :]
    lane = iota(facts.shape, 1)
    counts = jnp.where(lane < ctx_ref.shape[0], facts, 0.0)
    ahead = BLK * dot(below(groups), counts.astype(BF16))
    context.wait()
    base = context_row(ctx_ref) + ahead

    def fact(at):
        return jnp.sum(jnp.where(lane == at, facts, 0.0), axis=1, keepdims=True)

    turned = []
    for slot in range(CAP):
        hot = lane.astype(F32) == fact(16 + slot) - 1.0
        start = jnp.sum(jnp.where(hot, base, 0.0), axis=1, keepdims=True) + BLK * fact(18 + slot)
        turned.append(turns(start, sign))
    token_ref[...] = base[:8]
    for i in range(4):
        loads[i].wait()
        for g in range(i * step, (i + 1) * step):
            for slot in range(CAP):
                at = slot * 2 * BLK
                k = turned[slot](came_ref[g, at : at + BLK, :].astype(F32), g)
                both = jnp.concatenate([k, came_ref[g, at + BLK : at + 2 * BLK, :]], axis=0)
                to = (g * CAP + slot) * 2 * BLK
                out_ref[to : to + 2 * BLK, :] = dot(perm, both).astype(BF16)
        stores[i].start()
    wait_all(stores)


def finish(ctx, came, meta, after):
    shape = (came.shape[0] * META, HD)
    return pl.pallas_call(
        finish_kernel,
        in_specs=[HBM, HBM, VMEM, VMEM],
        out_specs=[HBM, VMEM],
        out_shape=[pltpu.HBM(shape, BF16), jax.ShapeDtypeStruct((8, HD), F32)],
        scratch_shapes=[
            pltpu.SMEM(ctx.shape, jnp.int32),
            pltpu.VMEM(came.shape, BF16),
            pltpu.VMEM(shape, BF16),
            pltpu.SemaphoreType.DMA((9,)),
        ],
        compiler_params=params(),
        cost_estimate=pl.CostEstimate(
            flops=80_000_000, bytes_accessed=3_000_000, transcendentals=0
        ),
        name="finish",
    )(*stay(ctx, came), meta, after)


def tree(values, op):
    while len(values) > 1:
        values = [op(values[i], values[i + 1]) for i in range(0, len(values), 2)]
    return values[0]


def merged(refs, tokens):
    add = lambda a, b: a + b
    stats = [ref[STAT:, :].astype(F32) for ref in refs]
    cs = [s[0:2] for s in stats]
    top = tree(cs, jnp.maximum)
    factors = [jnp.exp(c - top) for c in cs]
    total = tree([f * (s[2:4] + s[4:6]) for s, f in zip(stats, factors)], add)
    cols = jnp.concatenate(factors + [jnp.zeros((HD - 2 * len(refs), HD), F32)], axis=0).T
    halves = []
    for g in range(2):
        terms = [
            ref[g * HD : (g + 1) * HD, :].astype(F32) * cols[:, 2 * i + g : 2 * i + g + 1]
            for i, ref in enumerate(refs)
        ]
        halves.append(tree(terms, add))
    tok = jnp.concatenate([s[6 : 6 + 2 * tokens] for s in stats], axis=0)
    return halves, top, total, tok


def merge_kernel(*refs, tokens):
    out_ref = refs[-1]
    halves, top, total, tok = merged(refs[:-1], tokens)
    for g in range(2):
        out_ref[g * HD : (g + 1) * HD, :] = halves[g].astype(BF16)
    put_stats(out_ref, top, total, tok)


def merge(parts, tokens):
    return pl.pallas_call(
        functools.partial(merge_kernel, tokens=tokens),
        in_specs=[VMEM] * len(parts),
        out_specs=VMEM,
        out_shape=jax.ShapeDtypeStruct((payload_rows(len(parts) * tokens), HD), BF16),
        compiler_params=params(),
        name="merge",
    )(*parts)


def slot_token(slot, me):
    return me ^ (slot & 3) ^ (((slot >> 2) & 3) * 8) ^ ((slot >> 4) * 4)


def final_kernel(qr_ref, after_ref, *refs):
    out_ref, tok_out_ref = refs[-2:]
    me = lax.axis_index("wide")
    halves, top, total, tok = merged(refs[:-2], 16)
    keys = tok.astype(BF16)
    shape = (64, 64)
    to, of = iota(shape, 0), iota(shape, 1)
    moves = (to % 2 == of % 2) & (to // 2 == slot_token(of // 2, me))
    tok_out_ref[...] = dot(jnp.where(moves, 1.0, 0.0).astype(BF16), keys).astype(BF16)
    vals = pltpu.roll(tok, 63, 0).astype(BF16)
    cols = jnp.concatenate([top, total, jnp.zeros((HD - 4, HD), F32)], axis=0).T
    row, col = iota((HD, 64), 0), iota((HD, 64), 1)
    held = slot_token(col // 2, me)
    same = (col % 2 == 0) & (held % 16 == row % 16) & (held // 16 <= (row // 16) % 2)
    for g in range(2):
        s = dot_nt(qr_ref[g * HD : (g + 1) * HD, :], keys) * (HD ** (-0.5))
        s = jnp.where(same, s, MASKED)
        c, old = cols[:, g : g + 1], cols[:, 2 + g : 3 + g]
        m = jnp.maximum(c, jnp.max(s, axis=1, keepdims=True))
        f = jnp.exp(c - m)
        p = jnp.exp(s - m)
        whole = old * f + jnp.sum(p, axis=1, keepdims=True)
        o = ((halves[g] * f + dot(p.astype(BF16), vals)) / whole).astype(BF16)
        for h in range(4):
            head = g * 4 + h
            out_ref[:, head * HD : (head + 1) * HD] = o[h * 32 : (h + 1) * 32]


def final(qr, after, parts):
    return pl.pallas_call(
        final_kernel,
        in_specs=[VMEM] * (2 + len(parts)),
        out_specs=[VMEM, VMEM],
        out_shape=[
            jax.ShapeDtypeStruct((32, 8 * HD), BF16),
            jax.ShapeDtypeStruct((64, HD), BF16),
        ],
        compiler_params=params(),
        name="final",
    )(qr, after, *parts)


def exchange(value, axis, step):
    size = lax.axis_size(axis)
    return lax.ppermute(value, axis, [(i, i ^ step) for i in range(size)])


def add_bf16(a, b):
    return (a.astype(F32) + b.astype(F32)).astype(BF16)


def all_to_all(value):
    return lax.all_to_all(value, "wide", split_axis=0, concat_axis=0, tiled=True)


def local(
    prefill_rows,
    in_gain,
    key_weight,
    value_weight,
    key_gain,
    query_gain,
    block_request,
    block_target,
    context_lengths,
    kv_cache,
    decode_queries,
    decode_partials,
    decode_residual,
):
    wide_count = lax.axis_size("wide")
    row_count = context_lengths.shape[0]
    kgain = key_gain.reshape(1, HD)

    target = block_target.reshape(-1)
    meta, slots, part = describe(block_request, target, decode_partials, wide_count)
    meta = all_to_all(meta)

    first = part = add_bf16(part, exchange(part, "kvh", 1))
    part = add_bf16(part, exchange(part, "kvh", 2))
    decode_parts = [part, exchange(part, "kvh", 4)]

    weight, going = project(
        prefill_rows, in_gain, key_weight, value_weight, kgain, target, first, slots, wide_count,
    )
    going = hold(going, *decode_parts)
    came = all_to_all(going.reshape(wide_count, META, HD))
    payload, queries = attend(
        block_request, target, context_lengths, decode_queries.reshape(2 * row_count, -1),
        query_gain.reshape(1, HD), kv_cache,
        decode_residual, kgain, going, meta, weight, decode_parts,
    )
    parts = [payload] + [exchange(payload, "wide", step) for step in STAGES[0]]
    payload = merge(parts, 1)
    parts = [payload] + [exchange(payload, "wide", step) for step in STAGES[1]]
    payload = merge(parts, 4)
    parts = [payload] + [exchange(payload, "wide", step) for step in STAGES[2]]
    new_blocks, done = finish(context_lengths, came, meta, payload)
    attended, new = final(queries, done, parts)
    return (
        attended.reshape(2, row_count, -1),
        new_blocks.reshape(wide_count * CAP, BLK, 2, HD),
        new.reshape(2, row_count, 2, HD),
    )


def solution(mesh):
    placed = (
        P("wide", None),
        P(),
        P(None, "kvh"),
        P(None, "kvh"),
        P(),
        P(),
        P("wide"),
        P("wide", None),
        P(),
        P(None, None, "wide", "kvh"),
        P(None, None, "kvh"),
        P("kvh", None, None, None),
        P(),
    )
    return jax.shard_map(
        local,
        mesh=mesh,
        in_specs=placed,
        out_specs=(P(None, None, "kvh"), P("wide", None, None, "kvh"), P(None, None, None, "kvh")),
        check_vma=False,
    )
```
